128 devices in a mesh: space: 8 (over z_lo, y), tm: 16 (over z_hi, x, core).
Axes of the slice: x: 4, y: 4, z: 4 (z_hi: 2, z_lo: 2; z = z_hi * 2 + z_lo), core: 2. Of those that a mesh axis runs over, the one named last changes fastest.
Arguments:
- snapshots: bfloat16 [25600, 4096], P('space', 'tm')
- var_index: int32 [25600], P('space'), may hold values from 0 to 7, as said below
- modes: bfloat16 [25600, 64], P('space'), may hold values from -0.0390625 to 0.0390625
- retained: int32 [1], replicated, may hold values from 32 to 64
Outputs:
- gram: float32 [4096, 4096], P(None, 'tm')
- reduced: float32 [64, 4096], P('space', 'tm')
The draws below stay inside these ranges and needn't reach their ends.
Inputs may be any that keep to these rules, and one draw needn't show every extreme that they name: `var_index`: each variable labels the same number of rows, a 8-th of them.
All inputs are finite; a program needn't handle non-finite values.
Results may differ from the reference program's by a relative error of at most 0.0029.
Values may be sent and summed in bfloat16 or wider, within the bound.
A program may use at most 128 MiB of HBM per device.

```python
import jax
import jax.numpy as jnp
from jax import lax

VARS = 8
R = 64
SNAPS = 4096
ROWS = 25600


def labels(key):
    sub = jax.random.fold_in(key, 17)
    return jax.random.permutation(sub, jnp.arange(ROWS) % VARS).astype(jnp.int32)


def draw_var_index(key, part):
    shared = labels(key)
    return shared


def draw_snapshots(key, part):
    shared = labels(key)
    key = jax.random.fold_in(key, 5)
    first, second, third, fourth, fifth = jax.random.split(key, 5)
    offsets = jax.random.uniform(first, (VARS,), jnp.float32, -1.0, 1.0)
    spreads = jnp.exp(jax.random.uniform(second, (VARS,), jnp.float32, jnp.log(0.2), jnp.log(5.0)))
    magnitude = jax.random.uniform(fourth, (VARS,), jnp.float32, 0.6, 1.0)
    pointing = jnp.where(jax.random.uniform(fifth, (VARS,), jnp.float32, -1.0, 1.0) < 0.0, -1.0, 1.0)
    drift = spreads * magnitude * pointing
    row_pos = jnp.arange(ROWS).astype(jnp.float32) / jnp.float32(ROWS - 1)
    col_pos = jnp.arange(SNAPS).astype(jnp.float32) / jnp.float32(SNAPS - 1)
    noise = jax.random.normal(third, (ROWS, SNAPS), jnp.float32)
    row_ramp = 1.0 + 2.0 * row_pos
    col_ramp = 1.0 + 2.0 * col_pos
    shape_field = (col_pos[None, :] - 0.3) * (1.0 + row_pos[:, None]) + 1.5 * (row_pos[:, None] - 0.4)
    centre = offsets[shared][:, None] + drift[shared][:, None] * shape_field
    amplitude = spreads[shared][:, None] * row_ramp[:, None] * col_ramp[None, :]
    values = centre + amplitude * noise
    return values.astype(jnp.bfloat16)


def block_scale(stream_key, shape, shards, least, high):
    level, own = 1.0, jax.random.fold_in(stream_key, 6)
    for position, blocks in shards:
        heights = jnp.exp(jax.random.uniform(jax.random.fold_in(own, position), (blocks,), jnp.float32, least / len(shards), high / len(shards)))
        level = level * jnp.repeat(heights, shape[position] // blocks).reshape([-1 if axis == position else 1 for axis in range(len(shape))])
    return level


def normal_values(key, dims, deviation, limit, cuts=(), dtype=jnp.bfloat16):
    entries = deviation * jax.random.normal(key, dims, jnp.float32)
    if cuts:
        entries = entries * block_scale(key, dims, cuts, -0.22, 0.18)
    return jnp.clip(entries, -limit, limit).astype(dtype)


def setup_inputs(seed: int = 0) -> dict:
    arg_keys = jax.random.split(jax.random.key(seed), 5)
    snapshots = draw_snapshots(jax.random.fold_in(arg_keys[4], 71), 0)
    var_index = draw_var_index(jax.random.fold_in(arg_keys[4], 71), 0)
    modes = normal_values(arg_keys[2], (ROWS, R), ROWS ** -0.5, 0.0390625, ((0, 8),))
    retained = jax.random.randint(arg_keys[3], (1,), R // 2, R + 1).astype(jnp.int32)
    return dict(snapshots=snapshots, var_index=var_index, modes=modes, retained=retained)


def reference(snapshots, var_index, modes, retained):
    rows = snapshots.shape[0]
    snaps = snapshots.shape[1]
    count = rows // VARS * snaps
    data = snapshots.astype(jnp.float32)
    onehot = (var_index[:, None] == jnp.arange(VARS)[None, :]).astype(jnp.float32)
    row_sum = lax.optimization_barrier(jnp.sum(data, axis=1))
    mean = lax.optimization_barrier(jnp.sum(onehot * row_sum[:, None], axis=0)) / count
    mean_row = lax.optimization_barrier(jnp.sum(onehot * mean[None, :], axis=1))
    centered = data - mean_row[:, None]
    row_sq = lax.optimization_barrier(jnp.sum(centered * centered, axis=1))
    spread = jnp.sqrt(lax.optimization_barrier(jnp.sum(onehot * row_sq[:, None], axis=0)) / count + 1e-06)
    spread_row = lax.optimization_barrier(jnp.sum(onehot * spread[None, :], axis=1))
    scaled = (centered / spread_row[:, None]).astype(jnp.bfloat16)
    wide = scaled.astype(jnp.float32)
    gram = jnp.dot(wide.T, wide, precision=lax.Precision.HIGHEST) / jnp.sqrt(jnp.float32(rows))
    kept = jnp.where(jnp.arange(R)[None, :] < retained[0], modes, jnp.zeros_like(modes)).astype(jnp.bfloat16)
    reduced = jnp.dot(kept.astype(jnp.float32).T, wide, precision=lax.Precision.HIGHEST)
    return (gram, reduced)
```

```python
import jax
import jax.numpy as jnp
from jax import lax
from jax.experimental import pallas as pl
from jax.experimental.pallas import tpu as pltpu
from jax.sharding import PartitionSpec as P

MESH = pl.DeviceIdType.MESH
VARS = 8
NY, NX = 4, 4
NSPACE = 8
F32, BF16 = jnp.float32, jnp.bfloat16


def place():
    s, t = lax.axis_index("space"), lax.axis_index("tm")
    return s // NY, s % NY, t // 8, (t // 2) % NX, t % 2


def at(l, y, h, x, c):
    return (l * NY + y, h * 8 + x * 2 + c)


def nt(a, b):
    return lax.dot_general(a, b, (((1,), (1,)), ((), ())), preferred_element_type=F32)


def merge(tiles):
    n = sum(t[0:8] for t in tiles)
    total = sum(t[8:16] for t in tiles)
    mean = total / jnp.maximum(n, 1.0)
    squares = jnp.zeros_like(n)
    for t in tiles:
        off = t[8:16] / jnp.maximum(t[0:8], 1.0) - mean
        squares = squares + t[16:24] + t[0:8] * off * off
    return n, total, squares


def kernel(count, root, fk, x_ref, vi_ref, modes_ref, ret_ref, gram_ref, red_ref,
           xt, raw, rawe, relay, rawf, sc, sce, scf, hot, mean_l, inv_l, kept,
           tile1, tile2, got1, got2, part, cs, rs, redp, redr, piece, pieceT, ra, rt,
           bulk_s, bulk_r, st1_s, st1_r, st2_s, st2_r, rs_s, rs_r, rd_s, rd_r, ag_s, ra_r, rt_r):
    l, y, h, x, c = place()
    s = l * NY + y
    q = h * 2 + c
    rows = xt.shape[1]
    cols = xt.shape[0]
    ntile = rows // 128

    ring1 = [(dx, dc) for dx in range(NX) for dc in range(2) if (dx, dc) != (0, 0)]
    ring2 = [(dy, dl, dh) for dy in range(NY) for dl in range(2) for dh in range(2) if (dy, dl, dh) != (0, 0, 0)]

    def dev1(dx, dc, sign=1):
        return at(l, y, h, (x + sign * dx + NX) % NX, (c + dc) % 2)

    def dev2(dy, dl, dh, sign=1):
        return at((l + dl) % 2, (y + sign * dy + NY) % NY, (h + dh) % 2, x, c)

    barrier = pltpu.get_barrier_semaphore()
    for d in ring1:
        pl.semaphore_signal(barrier, inc=1, device_id=dev1(*d), device_id_type=MESH)
    for d in ring2:
        pl.semaphore_signal(barrier, inc=1, device_id=dev2(*d), device_id_type=MESH)

    for k in range(ntile):
        xt[:, 128 * k:128 * k + 128] = x_ref[128 * k:128 * k + 128, :].T

    pl.semaphore_wait(barrier, len(ring1) + len(ring2))

    def remote(src, dst, ss, rsem, dev):
        return pltpu.make_async_remote_copy(src, dst, ss, rsem, device_id=dev, device_id_type=MESH)

    fs_mine = pl.multiple_of((x // 2) * (rows - fk), 128)
    half = cols // 2
    to_f = [remote(xt.at[pl.ds(half * k, half), pl.ds(fs_mine, fk)], relay.at[pl.ds(half * k, half)],
                   bulk_s.at[k], bulk_r.at[k], at(l, y, h, (x + NX - 1) % NX, c)) for k in range(2)]
    to_e = remote(xt, rawe, bulk_s.at[2], bulk_r.at[2], at(l, y, h, (x + 1) % NX, c))
    to_z = remote(xt, raw.at[1], bulk_s.at[3], bulk_r.at[3], at(l, y, 1 - h, x, c))
    to_core = remote(xt, raw.at[0], bulk_s.at[4], bulk_r.at[4], at(l, y, h, x, 1 - c))
    for cp in to_f:
        cp.start()
    to_e.start()
    to_z.start()
    to_core.start()

    hot[...] = (vi_ref[...] == lax.broadcasted_iota(jnp.int32, (VARS, rows), 0)).astype(F32)

    def colsum(fn):
        def body(k, acc):
            blk = xt[pl.ds(pl.multiple_of(k * 16, 16), 16), :].astype(F32)
            return acc + fn(blk)
        acc = lax.fori_loop(0, cols // 16, body, jnp.zeros((16, rows), F32))
        return jnp.sum(acc, axis=0, keepdims=True)

    def wide(v):
        return jnp.broadcast_to(v, (VARS, 128))

    n1 = jnp.sum(hot[...], axis=1, keepdims=True) * cols
    sum1 = jnp.sum(hot[...] * colsum(lambda b: b), axis=1, keepdims=True)
    m1 = sum1 / jnp.maximum(n1, 1.0)
    mean_l[...] = jnp.sum(hot[...] * m1, axis=0, keepdims=True)

    def sq(b):
        d = b - mean_l[...]
        return d * d
    sq1 = jnp.sum(hot[...] * colsum(sq), axis=1, keepdims=True)
    tile1[0:8] = wide(n1)
    tile1[8:16] = wide(sum1)
    tile1[16:24] = wide(sq1)
    sends1 = [remote(tile1, got1.at[i], st1_s.at[i], st1_r.at[i], dev1(*d)) for i, d in enumerate(ring1)]
    for cp in sends1:
        cp.start()
    for k in range(ntile):
        kept[:, 128 * k:128 * k + 128] = modes_ref[128 * k:128 * k + 128, :].T
    keep = lax.broadcasted_iota(jnp.int32, kept.shape, 0) < ret_ref[0]
    kept[...] = jnp.where(keep, kept[...].astype(F32), 0.0).astype(BF16)
    for cp in sends1:
        cp.wait_recv()
    n2, sum2, sq2 = merge([tile1[...]] + [got1[i] for i in range(len(ring1))])
    tile2[0:8] = n2
    tile2[8:16] = sum2
    tile2[16:24] = sq2
    sends2 = [remote(tile2, got2.at[i], st2_s.at[i], st2_r.at[i], dev2(*d)) for i, d in enumerate(ring2)]
    for cp in sends2:
        cp.start()
    for cp in sends2:
        cp.wait_recv()
    _, sum3, sq3 = merge([tile2[...]] + [got2[i] for i in range(len(ring2))])
    mean = sum3 / count
    inv = 1.0 / jnp.sqrt(sq3 / count + 1e-06)
    mean_l[...] = jnp.sum(hot[...] * mean[:, 0:1], axis=0, keepdims=True)
    inv_l[...] = jnp.sum(hot[...] * inv[:, 0:1], axis=0, keepdims=True)

    def scale_to(dst, src):
        def body(k, _):
            r = pl.ds(pl.multiple_of(k * 16, 16), 16)
            dst[r, :] = ((src[r, :].astype(F32) - mean_l[...]) * inv_l[...]).astype(BF16)
            return 0
        lax.fori_loop(0, cols // 16, body, 0)

    scale_to(sc.at[q], xt)
    redp[...] = nt(kept[...], sc[q])

    fwd = [remote(relay.at[pl.ds(half * k, half)], rawf.at[pl.ds(half * k, half)],
                  bulk_s.at[5 + k], bulk_r.at[5 + k], at(l, y, h, (x + NX - 1) % NX, c)) for k in range(2)]
    to_core.wait_recv()
    scale_to(sc.at[h * 2 + (1 - c)], raw.at[0])
    for k in range(2):
        to_f[k].wait_recv()
        fwd[k].start()
    to_z.wait_recv()
    to_diag = remote(raw.at[1], raw.at[2], bulk_s.at[7], bulk_r.at[7], at(l, y, h, x, 1 - c))
    to_diag.start()
    scale_to(sc.at[(1 - h) * 2 + c], raw.at[1])
    to_e.wait_recv()
    scale_to(sce, rawe)
    to_diag.wait_recv()
    scale_to(sc.at[(1 - h) * 2 + (1 - c)], raw.at[2])

    def product(kind, right, lanes):
        def body(i, _):
            part[kind, pl.ds(pl.multiple_of(i * cols, cols), cols), :] = nt(sc[i, :, lanes], right)
            return 0
        lax.fori_loop(0, 4, body, 0)

    product(0, sc[q], slice(None))
    product(1, sce[...], slice(None))

    for k in range(2):
        fwd[k].wait_recv()
    fs = pl.multiple_of((((x + 2) % NX) // 2) * (rows - fk), 128)
    fl = pl.ds(fs, fk)
    over = 2 * fk - rows
    first = lax.broadcasted_iota(jnp.int32, (1, fk), 1) < over
    drop = jnp.logical_and(first, x < 2)
    f_inv = jnp.where(drop, 0.0, inv_l[:, fl])

    def fbody(k, _):
        r = pl.ds(pl.multiple_of(k * 16, 16), 16)
        scf[r, :] = ((rawf[r, :].astype(F32) - mean_l[:, fl]) * f_inv).astype(BF16)
        return 0
    lax.fori_loop(0, cols // 16, fbody, 0)
    product(2, scf[...], fl)

    ring3 = [(dl, dy) for dl in range(2) for dy in range(NY) if (dl, dy) != (0, 0)]
    for i in range(NSPACE):
        for kind in range(3):
            cs[i, kind] = part[kind, 128 * i:128 * i + 128, :].astype(BF16)
    rsend, dsend = [], []
    for i, (dl, dy) in enumerate(ring3):
        tl, ty = (l + dl) % 2, (y + dy) % NY
        ts = tl * NY + ty
        rsend.append(remote(cs.at[ts], rs.at[i], rs_s.at[i], rs_r.at[i], at(tl, ty, h, x, c)))
        dsend.append(remote(redp.at[pl.ds(pl.multiple_of(ts * 8, 8), 8)], redr.at[i], rd_s.at[i], rd_r.at[i],
                            at(tl, ty, h, x, c)))
    for a in rsend:
        a.start()
    for a in dsend:
        a.start()
    for a in rsend:
        a.wait_recv()
    for kind in range(3):
        tot = part[kind, pl.ds(pl.multiple_of(s * 128, 128), 128), :]
        for i in range(len(ring3)):
            tot = tot + rs[i, kind].astype(F32)
        tot = tot * (1.0 / root)
        piece[kind] = tot.astype(BF16)
        if kind > 0:
            pieceT[kind - 1] = tot.T.astype(BF16)

    own = s // 2
    oh, oc = own // 2, own % 2
    half_s = s % 2
    agsend = []
    for dl in range(2):
        for dy in range(NY):
            tl, ty = (l + dl) % 2, (y + dy) % NY
            k = dl * NY + dy
            dests = [at(tl, ty, h, x, c), at(tl, ty, h, (x + NX - 1) % NX, c), at(tl, ty, h, (x + 2) % NX, c)]
            for kind in range(3):
                if kind == 0 and k == 0:
                    continue
                cp = remote(piece.at[kind], ra.at[kind, s], ag_s.at[k * 5 + kind], ra_r.at[kind, s], dests[kind])
                cp.start()
                agsend.append(cp)
            for kind in range(2):
                cp = remote(pieceT.at[kind], rt.at[kind, q, half_s], ag_s.at[k * 5 + 3 + kind], rt_r.at[kind, q, half_s],
                            at(tl, ty, oh, x, oc))
                if k == 0:
                    lc = pltpu.make_async_copy(pieceT.at[kind], rt.at[kind, q, half_s], rt_r.at[kind, q, half_s])

                    @pl.when(own == q)
                    def _():
                        lc.start()

                    @pl.when(own != q)
                    def _():
                        cp.start()
                else:
                    cp.start()
                    agsend.append(cp)
    ra[0, s] = piece[0]

    for a in dsend:
        a.wait_recv()
    tot = redp[pl.ds(pl.multiple_of(s * 8, 8), 8), :]
    for i in range(len(ring3)):
        tot = tot + redr[i]
    red_ref[...] = tot

    def got(ref, sem):
        pltpu.make_async_copy(ref, ref, sem).wait()

    def rows_of(hc, xx):
        return ((hc // 2) * 8 + xx * 2 + hc % 2) * cols

    for kind in range(3):
        xx = [x, (x + 1) % NX, (x + 2) % NX][kind]
        for j in range(NSPACE):
            if kind == 0:
                @pl.when(s != j)
                def _():
                    got(ra.at[0, j], ra_r.at[0, j])
            else:
                got(ra.at[kind, j], ra_r.at[kind, j])
            r0 = pl.multiple_of(rows_of(j // 2, xx) + (j % 2) * 128, 128)
            gram_ref[pl.ds(r0, 128), :] = ra[kind, j].astype(F32)
    for kind in range(2):
        xx = [(x + NX - 1) % NX, (x + 2) % NX][kind]
        for hc in range(4):
            r0 = pl.multiple_of(rows_of(hc, xx), cols)
            for b in range(2):
                got(rt.at[kind, hc, b], rt_r.at[kind, hc, b])
                val = rt[kind, hc, b].astype(F32)
                if kind == 1:
                    val = val + gram_ref[pl.ds(r0, cols), 128 * b:128 * b + 128]
                gram_ref[pl.ds(r0, cols), 128 * b:128 * b + 128] = val

    for cp in to_f + fwd + [to_e, to_z, to_core, to_diag] + sends1 + sends2 + rsend + dsend + agsend:
        cp.wait_send()
    for kind in range(2):
        @pl.when(own != q)
        def _():
            remote(pieceT.at[kind], rt.at[kind, q, half_s], ag_s.at[3 + kind], rt_r.at[kind, q, half_s],
                   at(l, y, oh, x, oc)).wait_send()


def local(snapshots, var_index, modes, retained):
    rows, cols = snapshots.shape
    n_space, n_time = lax.axis_size("space"), lax.axis_size("tm")
    total_rows = rows * n_space
    count = float(total_rows // VARS * (cols * n_time))
    root = float(total_rows) ** 0.5
    r = modes.shape[1]
    fk = (rows // 128 + 1) // 2 * 128
    dma = pltpu.SemaphoreType.DMA

    def body(*refs):
        kernel(count, root, fk, *refs)

    vmem = pl.BlockSpec(memory_space=pltpu.VMEM)
    return pl.pallas_call(
        body,
        name="gram",
        out_shape=(jax.ShapeDtypeStruct((cols * n_time, cols), F32), jax.ShapeDtypeStruct((r // n_space, cols), F32)),
        in_specs=[vmem, vmem, vmem, pl.BlockSpec(memory_space=pltpu.SMEM)],
        out_specs=(vmem, vmem),
        scratch_shapes=[
            pltpu.VMEM((cols, rows), BF16),
            pltpu.VMEM((3, cols, rows), BF16),
            pltpu.VMEM((cols, rows), BF16),
            pltpu.VMEM((cols, fk), BF16),
            pltpu.VMEM((cols, fk), BF16),
            pltpu.VMEM((4, cols, rows), BF16),
            pltpu.VMEM((cols, rows), BF16),
            pltpu.VMEM((cols, fk), BF16),
            pltpu.VMEM((VARS, rows), F32),
            pltpu.VMEM((1, rows), F32),
            pltpu.VMEM((1, rows), F32),
            pltpu.VMEM((r, rows), BF16),
            pltpu.VMEM((24, 128), F32),
            pltpu.VMEM((24, 128), F32),
            pltpu.VMEM((7, 24, 128), F32),
            pltpu.VMEM((15, 24, 128), F32),
            pltpu.VMEM((3, 4 * cols, cols), F32),
            pltpu.VMEM((8, 3, 128, cols), BF16),
            pltpu.VMEM((7, 3, 128, cols), BF16),
            pltpu.VMEM((r, cols), F32),
            pltpu.VMEM((7, 8, cols), F32),
            pltpu.VMEM((3, 128, cols), BF16),
            pltpu.VMEM((2, cols, 128), BF16),
            pltpu.VMEM((3, 8, 128, cols), BF16),
            pltpu.VMEM((2, 4, 2, cols, 128), BF16),
            dma((8,)), dma((8,)), dma((7,)), dma((7,)), dma((15,)), dma((15,)),
            dma((7,)), dma((7,)), dma((7,)), dma((7,)), dma((40,)), dma((3, 8)), dma((2, 4, 2)),
        ],
        compiler_params=pltpu.CompilerParams(
            collective_id=0, has_side_effects=True, vmem_limit_bytes=60 * 2 ** 20),
    )(snapshots, var_index.reshape(1, rows), modes, retained)


def solution(mesh):
    return jax.shard_map(
        local,
        mesh=mesh,
        in_specs=(P("space", "tm"), P("space"), P("space", None), P()),
        out_specs=(P(None, "tm"), P("space", "tm")),
        check_vma=False,
    )
```

```python
import jax
import jax.numpy as jnp
from jax import lax
from jax.experimental import pallas as pl
from jax.experimental.pallas import tpu as pltpu
from jax.sharding import PartitionSpec as P

MESH = pl.DeviceIdType.MESH
VARS = 8
NY, NX = 4, 4
NSPACE = 8
F32, BF16 = jnp.float32, jnp.bfloat16


def place():
    s, t = lax.axis_index("space"), lax.axis_index("tm")
    return s // NY, s % NY, t // 8, (t // 2) % NX, t % 2


def at(l, y, h, x, c):
    return (l * NY + y, h * 8 + x * 2 + c)


def nt(a, b):
    return lax.dot_general(a, b, (((1,), (1,)), ((), ())), preferred_element_type=F32)


def merge(tiles):
    n = sum(t[0:8] for t in tiles)
    total = sum(t[8:16] for t in tiles)
    mean = total / jnp.maximum(n, 1.0)
    squares = jnp.zeros_like(n)
    for t in tiles:
        off = t[8:16] / jnp.maximum(t[0:8], 1.0) - mean
        squares = squares + t[16:24] + t[0:8] * off * off
    return n, total, squares


def kernel(count, root, fk, x_ref, vi_ref, modes_ref, ret_ref, ra, rt, red_ref,
           xt, raw, rawe, relay, rawf, sc, sce, scf, hot, mean_l, inv_l, kept,
           tile1, tile2, got1, got2, part, cs, rs, redp, redr, piece, pieceT,
           bulk_s, bulk_r, st1_s, st1_r, st2_s, st2_r, rs_s, rs_r, rd_s, rd_r, ag_s, ra_r, rt_r):
    l, y, h, x, c = place()
    s = l * NY + y
    q = h * 2 + c
    rows = xt.shape[1]
    cols = xt.shape[0]
    ntile = rows // 128

    ring1 = [(dx, dc) for dx in range(NX) for dc in range(2) if (dx, dc) != (0, 0)]
    ring2 = [(dy, dl, dh) for dy in range(NY) for dl in range(2) for dh in range(2) if (dy, dl, dh) != (0, 0, 0)]

    def dev1(dx, dc, sign=1):
        return at(l, y, h, (x + sign * dx + NX) % NX, (c + dc) % 2)

    def dev2(dy, dl, dh, sign=1):
        return at((l + dl) % 2, (y + sign * dy + NY) % NY, (h + dh) % 2, x, c)

    barrier = pltpu.get_barrier_semaphore()
    for d in ring1:
        pl.semaphore_signal(barrier, inc=1, device_id=dev1(*d), device_id_type=MESH)
    for d in ring2:
        pl.semaphore_signal(barrier, inc=1, device_id=dev2(*d), device_id_type=MESH)

    for k in range(ntile):
        xt[:, 128 * k:128 * k + 128] = x_ref[128 * k:128 * k + 128, :].T

    pl.semaphore_wait(barrier, len(ring1) + len(ring2))

    def remote(src, dst, ss, rsem, dev):
        return pltpu.make_async_remote_copy(src, dst, ss, rsem, device_id=dev, device_id_type=MESH)

    fs_mine = pl.multiple_of((x // 2) * (rows - fk), 128)
    cuts = [0, 32, 128, cols]
    parts = [pl.ds(lo, hi - lo) for lo, hi in zip(cuts, cuts[1:])]
    to_f, to_e, to_z, to_core, to_diag, fwd = [], [], [], [], [], []
    for k, r in enumerate(parts):
        left = at(l, y, h, (x + NX - 1) % NX, c)
        core = at(l, y, h, x, 1 - c)
        to_f.append(remote(xt.at[r, pl.ds(fs_mine, fk)], relay.at[r], bulk_s.at[0, k], bulk_r.at[0, k], left))
        to_e.append(remote(xt.at[r], rawe.at[r], bulk_s.at[1, k], bulk_r.at[1, k], at(l, y, h, (x + 1) % NX, c)))
        to_z.append(remote(xt.at[r], raw.at[1, r], bulk_s.at[2, k], bulk_r.at[2, k], at(l, y, 1 - h, x, c)))
        to_core.append(remote(xt.at[r], raw.at[0, r], bulk_s.at[3, k], bulk_r.at[3, k], core))
        to_diag.append(remote(raw.at[1, r], raw.at[2, r], bulk_s.at[4, k], bulk_r.at[4, k], core))
        fwd.append(remote(relay.at[r], rawf.at[r], bulk_s.at[5, k], bulk_r.at[5, k], left))

    def send_part(k):
        for cp in (to_f[k], to_e[k], to_z[k], to_core[k]):
            cp.start()

    send_part(0)

    hot[...] = (vi_ref[...][None, :] == lax.broadcasted_iota(jnp.int32, (VARS, rows), 0)).astype(F32)

    def colsum(fn):
        def body(k, acc):
            blk = xt[pl.ds(pl.multiple_of(k * 16, 16), 16), :].astype(F32)
            return acc + fn(blk)
        acc = lax.fori_loop(0, cols // 16, body, jnp.zeros((16, rows), F32))
        return jnp.sum(acc, axis=0, keepdims=True)

    def wide(v):
        return jnp.broadcast_to(v, (VARS, 128))

    n1 = jnp.sum(hot[...], axis=1, keepdims=True) * cols
    sum1 = jnp.sum(hot[...] * colsum(lambda b: b), axis=1, keepdims=True)
    m1 = sum1 / jnp.maximum(n1, 1.0)
    mean_l[...] = jnp.sum(hot[...] * m1, axis=0, keepdims=True)

    def sq(b):
        d = b - mean_l[...]
        return d * d
    sq1 = jnp.sum(hot[...] * colsum(sq), axis=1, keepdims=True)
    tile1[0:8] = wide(n1)
    tile1[8:16] = wide(sum1)
    tile1[16:24] = wide(sq1)
    sends1 = [remote(tile1, got1.at[i], st1_s.at[i], st1_r.at[i], dev1(*d)) for i, d in enumerate(ring1)]
    for cp in sends1:
        cp.start()
    send_part(1)
    keep = lax.broadcasted_iota(jnp.int32, kept.shape, 0) < ret_ref[0]
    kept[...] = jnp.where(keep, modes_ref[...].astype(F32), 0.0).astype(BF16)
    for cp in sends1:
        cp.wait_recv()
    n2, sum2, sq2 = merge([tile1[...]] + [got1[i] for i in range(len(ring1))])
    tile2[0:8] = n2
    tile2[8:16] = sum2
    tile2[16:24] = sq2
    sends2 = [remote(tile2, got2.at[i], st2_s.at[i], st2_r.at[i], dev2(*d)) for i, d in enumerate(ring2)]
    for cp in sends2:
        cp.start()
    send_part(2)
    for cp in sends2:
        cp.wait_recv()
    _, sum3, sq3 = merge([tile2[...]] + [got2[i] for i in range(len(ring2))])
    mean = sum3 / count
    inv = 1.0 / jnp.sqrt(sq3 / count + 1e-06)
    mean_l[...] = jnp.sum(hot[...] * mean[:, 0:1], axis=0, keepdims=True)
    inv_l[...] = jnp.sum(hot[...] * inv[:, 0:1], axis=0, keepdims=True)

    def scale_to(dst, src, lo, n, m, v):
        def body(k, _):
            r = pl.ds(pl.multiple_of(lo + k * 16, 16), 16)
            dst[r, :] = ((src[r, :].astype(F32) - m) * v).astype(BF16)
            return 0
        lax.fori_loop(0, n // 16, body, 0)

    def scale(dst, src, lo=0, n=cols):
        scale_to(dst, src, lo, n, mean_l[...], inv_l[...])

    fs = pl.multiple_of((((x + 2) % NX) // 2) * (rows - fk), 128)
    fl = pl.ds(fs, fk)
    over = 2 * fk - rows
    first = lax.broadcasted_iota(jnp.int32, (1, fk), 1) < over
    drop = jnp.logical_and(first, x < 2)
    f_mean = mean_l[:, fl]
    f_inv = jnp.where(drop, 0.0, inv_l[:, fl])

    def product(kind, i, right, lanes):
        part[kind, pl.ds(pl.multiple_of(i * cols, cols), cols), :] = nt(sc[i, :, lanes], right)

    every = slice(None)
    q1, q2, q3 = h * 2 + (1 - c), (1 - h) * 2 + c, (1 - h) * 2 + (1 - c)
    scale(sc.at[q], xt)
    redp[...] = nt(kept[...], sc[q])
    product(0, q, sc[q], every)
    for k in range(len(parts)):
        to_core[k].wait_recv()
    scale(sc.at[q1], raw.at[0])
    product(0, q1, sc[q], every)

    for k in range(len(parts)):
        lo, n = cuts[k], cuts[k + 1] - cuts[k]
        to_f[k].wait_recv()
        fwd[k].start()
        to_z[k].wait_recv()
        to_diag[k].start()
        scale(sc.at[q2], raw.at[1], lo, n)
        to_e[k].wait_recv()
        scale(sce, rawe, lo, n)
        to_diag[k].wait_recv()
        scale(sc.at[q3], raw.at[2], lo, n)
        if k > 0:
            fwd[k - 1].wait_recv()
            scale_to(scf, rawf, cuts[k - 1], cuts[k] - cuts[k - 1], f_mean, f_inv)
    product(0, q2, sc[q], every)
    product(0, q3, sc[q], every)
    for i in range(4):
        product(1, i, sce[...], every)
    fwd[-1].wait_recv()
    scale_to(scf, rawf, cuts[-2], cuts[-1] - cuts[-2], f_mean, f_inv)
    for i in range(4):
        product(2, i, scf[...], fl)

    ring3 = [(dl, dy) for dl in range(2) for dy in range(NY) if (dl, dy) != (0, 0)]
    for i in range(NSPACE):
        for kind in range(3):
            cs[i, kind] = part[kind, 128 * i:128 * i + 128, :].astype(BF16)
    rsend, dsend = [], []
    for i, (dl, dy) in enumerate(ring3):
        tl, ty = (l + dl) % 2, (y + dy) % NY
        ts = tl * NY + ty
        rsend.append(remote(cs.at[ts], rs.at[i], rs_s.at[i], rs_r.at[i], at(tl, ty, h, x, c)))
        dsend.append(remote(redp.at[pl.ds(pl.multiple_of(ts * 8, 8), 8)], redr.at[i], rd_s.at[i], rd_r.at[i],
                            at(tl, ty, h, x, c)))
    for a in rsend:
        a.start()
    for a in dsend:
        a.start()
    for a in rsend:
        a.wait_recv()
    for kind in range(3):
        tot = part[kind, pl.ds(pl.multiple_of(s * 128, 128), 128), :]
        for i in range(len(ring3)):
            tot = tot + rs[i, kind].astype(F32)
        tot = tot * (1.0 / root)
        piece[kind] = tot.astype(BF16)
        if kind > 0:
            pieceT[kind - 1] = tot.T.astype(BF16)

    own = s // 2
    oh, oc = own // 2, own % 2
    half_s = s % 2
    agsend = []
    for dl in range(2):
        for dy in range(NY):
            tl, ty = (l + dl) % 2, (y + dy) % NY
            k = dl * NY + dy
            dests = [at(tl, ty, h, x, c), at(tl, ty, h, (x + NX - 1) % NX, c), at(tl, ty, h, (x + 2) % NX, c)]
            for kind in range(3):
                if kind == 0 and k == 0:
                    continue
                cp = remote(piece.at[kind], ra.at[kind, s], ag_s.at[k * 5 + kind], ra_r.at[kind, s], dests[kind])
                cp.start()
                agsend.append(cp)
            for kind in range(2):
                cp = remote(pieceT.at[kind], rt.at[kind, q, half_s], ag_s.at[k * 5 + 3 + kind], rt_r.at[kind, q, half_s],
                            at(tl, ty, oh, x, oc))
                if k == 0:
                    lc = pltpu.make_async_copy(pieceT.at[kind], rt.at[kind, q, half_s], rt_r.at[kind, q, half_s])

                    @pl.when(own == q)
                    def _():
                        lc.start()

                    @pl.when(own != q)
                    def _():
                        cp.start()
                else:
                    cp.start()
                    agsend.append(cp)
    mine = pltpu.make_async_copy(piece.at[0], ra.at[0, s], ra_r.at[0, s])
    mine.start()

    for a in dsend:
        a.wait_recv()
    tot = redp[pl.ds(pl.multiple_of(s * 8, 8), 8), :]
    for i in range(len(ring3)):
        tot = tot + redr[i]
    red_ref[...] = tot

    def got(ref, sem):
        pltpu.make_async_copy(ref, ref, sem).wait()

    for kind in range(3):
        for j in range(NSPACE):
            got(ra.at[kind, j], ra_r.at[kind, j])
    for kind in range(2):
        for hc in range(4):
            for b in range(2):
                got(rt.at[kind, hc, b], rt_r.at[kind, hc, b])

    for cp in to_f + fwd + to_e + to_z + to_core + to_diag + sends1 + sends2 + rsend + dsend + agsend:
        cp.wait_send()
    for kind in range(2):
        @pl.when(own != q)
        def _():
            remote(pieceT.at[kind], rt.at[kind, q, half_s], ag_s.at[3 + kind], rt_r.at[kind, q, half_s],
                   at(l, y, oh, x, oc)).wait_send()


def assemble(x_ref, ra, rt, red_in, gram_ref, red_ref):
    k = pl.program_id(0)
    red_ref[...] = red_in[...]
    cols = gram_ref.shape[3]
    for kind in range(3):
        @pl.when(k == kind)
        def _():
            for j in range(NSPACE):
                rows = pl.ds((j % 4) * 128, 128)
                gram_ref[j // 4, 0, rows, :] = ra[kind, j].astype(F32)
    for kind in range(2):
        @pl.when(k == 3 - kind)
        def _():
            for hc in range(4):
                rows = pl.ds((hc % 2) * cols, cols)
                for b in range(2):
                    lanes = pl.ds(128 * b, 128)
                    val = rt[kind, hc, b].astype(F32)
                    if kind == 1:
                        val = val + gram_ref[hc // 2, 0, rows, lanes]
                    gram_ref[hc // 2, 0, rows, lanes] = val


def local(snapshots, var_index, modes, retained):
    rows, cols = snapshots.shape
    n_space, n_time = lax.axis_size("space"), lax.axis_size("tm")
    total_rows = rows * n_space
    count = float(total_rows // VARS * (cols * n_time))
    root = float(total_rows) ** 0.5
    r = modes.shape[1]
    fk = (rows // 128 + 1) // 2 * 128
    dma = pltpu.SemaphoreType.DMA

    def body(*refs):
        kernel(count, root, fk, *refs)

    vmem = pl.BlockSpec(memory_space=pltpu.VMEM)
    ra, rt, red = pl.pallas_call(
        body,
        name="gram",
        out_shape=(jax.ShapeDtypeStruct((3, 8, 128, cols), BF16), jax.ShapeDtypeStruct((2, 4, 2, cols, 128), BF16),
                   jax.ShapeDtypeStruct((r // n_space, cols), F32)),
        in_specs=[vmem, vmem, vmem, pl.BlockSpec(memory_space=pltpu.SMEM)],
        out_specs=(pl.BlockSpec(memory_space=pl.ANY), pl.BlockSpec(memory_space=pl.ANY), vmem),
        scratch_shapes=[
            pltpu.VMEM((cols, rows), BF16),
            pltpu.VMEM((3, cols, rows), BF16),
            pltpu.VMEM((cols, rows), BF16),
            pltpu.VMEM((cols, fk), BF16),
            pltpu.VMEM((cols, fk), BF16),
            pltpu.VMEM((4, cols, rows), BF16),
            pltpu.VMEM((cols, rows), BF16),
            pltpu.VMEM((cols, fk), BF16),
            pltpu.VMEM((VARS, rows), F32),
            pltpu.VMEM((1, rows), F32),
            pltpu.VMEM((1, rows), F32),
            pltpu.VMEM((r, rows), BF16),
            pltpu.VMEM((24, 128), F32),
            pltpu.VMEM((24, 128), F32),
            pltpu.VMEM((7, 24, 128), F32),
            pltpu.VMEM((15, 24, 128), F32),
            pltpu.VMEM((3, 4 * cols, cols), F32),
            pltpu.VMEM((8, 3, 128, cols), BF16),
            pltpu.VMEM((7, 3, 128, cols), BF16),
            pltpu.VMEM((r, cols), F32),
            pltpu.VMEM((7, 8, cols), F32),
            pltpu.VMEM((3, 128, cols), BF16),
            pltpu.VMEM((2, cols, 128), BF16),
            dma((6, 3)), dma((6, 3)), dma((7,)), dma((7,)), dma((15,)), dma((15,)),
            dma((7,)), dma((7,)), dma((7,)), dma((7,)), dma((40,)), dma((3, 8)), dma((2, 4, 2)),
        ],
        compiler_params=pltpu.CompilerParams(
            collective_id=0, has_side_effects=True, vmem_limit_bytes=60 * 2 ** 20),
    )(snapshots, var_index, modes.T, retained)
    x = ((lax.axis_index("tm") // 2) % NX).reshape(1)
    gram, red = pl.pallas_call(
        assemble,
        name="columns",
        grid_spec=pltpu.PrefetchScalarGridSpec(
            num_scalar_prefetch=1,
            grid=(NX,),
            in_specs=[pl.BlockSpec(ra.shape, lambda k, x: (0,) * 4), pl.BlockSpec(rt.shape, lambda k, x: (0,) * 5),
                      pl.BlockSpec(red.shape, lambda k, x: (0, 0))],
            out_specs=[pl.BlockSpec((2, 1, 2 * cols, cols), lambda k, x: (0, (x[0] + k) % NX, 0, 0)),
                       pl.BlockSpec(red.shape, lambda k, x: (0, 0))],
        ),
        out_shape=(jax.ShapeDtypeStruct((2, NX, 2 * cols, cols), F32), jax.ShapeDtypeStruct(red.shape, F32)),
        compiler_params=pltpu.CompilerParams(vmem_limit_bytes=32 * 2 ** 20),
    )(x, ra, rt, red)
    return gram.reshape(cols * n_time, cols), red


def solution(mesh):
    return jax.shard_map(
        local,
        mesh=mesh,
        in_specs=(P("space", "tm"), P("space"), P("space", None), P()),
        out_specs=(P(None, "tm"), P("space", "tm")),
        check_vma=False,
    )
```

```python
import jax
import jax.numpy as jnp
from jax import lax
from jax.experimental import pallas as pl
from jax.experimental.pallas import tpu as pltpu
from jax.sharding import PartitionSpec as P

MESH = pl.DeviceIdType.MESH
VARS = 8
NY, NX = 4, 4
F32, BF16 = jnp.float32, jnp.bfloat16


def place():
    s, t = lax.axis_index("space"), lax.axis_index("tm")
    return s // NY, s % NY, t // 8, (t // 2) % NX, t % 2


def at(l, y, h, x, c):
    return (l * NY + y, h * 8 + x * 2 + c)


def nt(a, b):
    return lax.dot_general(a, b, (((1,), (1,)), ((), ())), preferred_element_type=F32)


def merge(tiles):
    n = sum(t[0:8] for t in tiles)
    total = sum(t[8:16] for t in tiles)
    mean = total / jnp.maximum(n, 1.0)
    squares = jnp.zeros_like(n)
    for t in tiles:
        off = t[8:16] / jnp.maximum(t[0:8], 1.0) - mean
        squares = squares + t[16:24] + t[0:8] * off * off
    return n, total, squares


def role(g, y):
    two, odd = y // 2, y % 2
    if g == 0:
        return 0, 0, two, odd
    if g in (1, 3):
        return 0, 1 + odd, two, g // 2
    if g == 4:
        return 1, 1 + odd, two, 1 - two
    last = g // 3
    return (1, 0, last, odd) if two == 0 else (1, 1 + odd, last, last)


SETS = 6
MIXED = (2, 5)
EARLY = 3
YFIRST = (3, 5)
CUTS = (0, 32, 128, 160, 192, 224, 256)
ZCUTS = (0, 64, 128, 160, 192, 224, 256)


def kernel(count, root, fk, x_ref, vi_ref, modes_ref, ret_ref, fin, red_ref,
           xt, raw, rawe, relay, rawf, near, far, ef, hot, mean_l, inv_l, kept,
           tile1, tile2, got1, got2, ps, cs, rs, tmp, r2, redp, redr, pc, pt,
           bulk_s, bulk_r, st1_s, st1_r, st2_s, st2_r, rs_s, rs_r, r2_s, r2_r, rd_s, rd_r, a_s, fin_r, b_s, b_r,
           ay_s, al_s, late_r, rd, d_s, d_r):
    l, y, h, x, c = place()
    s = l * NY + y
    rows = xt.shape[1]
    cols = xt.shape[0]
    ntile = rows // 128
    drain = []

    ring1 = [(dx, dc) for dx in range(NX) for dc in range(2) if (dx, dc) != (0, 0)]
    ring2 = [(dy, dl, dh) for dy in range(NY) for dl in range(2) for dh in range(2) if (dy, dl, dh) != (0, 0, 0)]

    def dev1(dx, dc):
        return at(l, y, h, (x + dx) % NX, (c + dc) % 2)

    def dev2(dy, dl, dh):
        return at((l + dl) % 2, (y + dy) % NY, (h + dh) % 2, x, c)

    barrier = pltpu.get_barrier_semaphore()
    for d in ring1:
        pl.semaphore_signal(barrier, inc=1, device_id=dev1(*d), device_id_type=MESH)
    for d in ring2:
        pl.semaphore_signal(barrier, inc=1, device_id=dev2(*d), device_id_type=MESH)

    def turn(half):
        for k in range(ntile):
            xt[128 * half:128 * half + 128, 128 * k:128 * k + 128] = x_ref[128 * k:128 * k + 128, 128 * half:128 * half + 128].T

    turn(0)
    pl.semaphore_wait(barrier, len(ring1) + len(ring2))

    def remote(src, dst, ss, rsem, dev):
        return pltpu.make_async_remote_copy(src, dst, ss, rsem, device_id=dev, device_id_type=MESH)

    def go(*copies):
        for cp in copies:
            cp.start()
            drain.append(cp)

    fs_mine = pl.multiple_of((x // 2) * (rows - fk), 128)
    parts = [pl.ds(lo, hi - lo) for lo, hi in zip(CUTS, CUTS[1:])]
    to_f, to_e, to_z, to_core, to_diag, fwd = [], [], [], [], [], []
    left, core = at(l, y, h, (x + NX - 1) % NX, c), at(l, y, h, x, 1 - c)
    for k, r in enumerate(parts):
        to_f.append(remote(xt.at[r, pl.ds(fs_mine, fk)], relay.at[r], bulk_s.at[0, k], bulk_r.at[0, k], left))
        to_e.append(remote(xt.at[r], rawe.at[r], bulk_s.at[1, k], bulk_r.at[1, k], at(l, y, h, (x + 1) % NX, c)))
        fwd.append(remote(relay.at[r], rawf.at[r], bulk_s.at[5, k], bulk_r.at[5, k], left))
    for k, r in enumerate([pl.ds(lo, hi - lo) for lo, hi in zip(ZCUTS, ZCUTS[1:])]):
        to_z.append(remote(xt.at[r], raw.at[1, r], bulk_s.at[2, k], bulk_r.at[2, k], at(l, y, 1 - h, x, c)))
        to_diag.append(remote(raw.at[1, r], raw.at[2, r], bulk_s.at[4, k], bulk_r.at[4, k], core))
    to_core = remote(xt, raw.at[0], bulk_s.at[3, 0], bulk_r.at[3, 0], core)

    go(to_f[0], to_e[0], to_z[0])
    turn(1)
    go(to_core)

    hot[...] = (vi_ref[...][None, :] == lax.broadcasted_iota(jnp.int32, (VARS, rows), 0)).astype(F32)

    def colsum(fn):
        def body(k, acc):
            blk = xt[pl.ds(pl.multiple_of(k * 16, 16), 16), :].astype(F32)
            return acc + fn(blk)
        acc = lax.fori_loop(0, cols // 16, body, jnp.zeros((16, rows), F32))
        return jnp.sum(acc, axis=0, keepdims=True)

    def wide(v):
        return jnp.broadcast_to(v, (VARS, 128))

    n1 = jnp.sum(hot[...], axis=1, keepdims=True) * cols
    sum1 = jnp.sum(hot[...] * colsum(lambda b: b), axis=1, keepdims=True)
    m1 = sum1 / jnp.maximum(n1, 1.0)
    mean_l[...] = jnp.sum(hot[...] * m1, axis=0, keepdims=True)

    def sq(b):
        d = b - mean_l[...]
        return d * d
    sq1 = jnp.sum(hot[...] * colsum(sq), axis=1, keepdims=True)
    tile1[0:8] = wide(n1)
    tile1[8:16] = wide(sum1)
    tile1[16:24] = wide(sq1)
    sends1 = [remote(tile1, got1.at[i], st1_s.at[i], st1_r.at[i], dev1(*d)) for i, d in enumerate(ring1)]
    go(*sends1)
    go(to_f[1], to_e[1])
    keep = lax.broadcasted_iota(jnp.int32, kept.shape, 0) < ret_ref[0]
    kept[...] = jnp.where(keep, modes_ref[...].astype(F32), 0.0).astype(BF16)
    for half in range(2):
        ef[half, 128:256, :] = jnp.zeros((128, rows), BF16)
    for cp in sends1:
        cp.wait_recv()
    to_f[0].wait_recv()
    go(fwd[0])
    n2, sum2, sq2 = merge([tile1[...]] + [got1[i] for i in range(len(ring1))])
    tile2[0:8] = n2
    tile2[8:16] = sum2
    tile2[16:24] = sq2
    sends2 = [remote(tile2, got2.at[i], st2_s.at[i], st2_r.at[i], dev2(*d)) for i, d in enumerate(ring2)]
    go(*sends2)
    go(to_z[1])
    to_f[1].wait_recv()
    go(fwd[1], to_e[2], *to_f[2:])
    for cp in sends2:
        cp.wait_recv()
    _, sum3, sq3 = merge([tile2[...]] + [got2[i] for i in range(len(ring2))])
    mean = sum3 / count
    inv = 1.0 / jnp.sqrt(sq3 / count + 1e-06)
    mean_l[...] = jnp.sum(hot[...] * mean[:, 0:1], axis=0, keepdims=True)
    inv_l[...] = jnp.sum(hot[...] * inv[:, 0:1], axis=0, keepdims=True)
    go(to_z[2])

    def scale_to(dst, dlo, src, lo, n, m, v):
        def body(k, _):
            a = pl.multiple_of(k * 16, 16)
            dst[pl.ds(dlo + a, 16), :] = ((src[pl.ds(lo + a, 16), :].astype(F32) - m) * v).astype(BF16)
            return 0
        lax.fori_loop(0, n // 16, body, 0)

    def scale(dst, dlo, src, lo, n):
        scale_to(dst, dlo, src, lo, n, mean_l[...], inv_l[...])

    fs = pl.multiple_of((((x + 2) % NX) // 2) * (rows - fk), 128)
    fl = pl.ds(fs, fk)
    over = 2 * fk - rows
    first = lax.broadcasted_iota(jnp.int32, (1, fk), 1) < over
    drop = jnp.logical_and(first, x < 2)

    def scale_f(k):
        half, lo = CUTS[k] // 128, CUTS[k] % 128
        scale_to(ef.at[half, :, fl], 128 + lo, rawf, CUTS[k], CUTS[k + 1] - CUTS[k], mean_l[:, fl],
                 jnp.where(drop, 0.0, inv_l[:, fl]))

    def scale_z(k):
        half, lo, n = ZCUTS[k] // 128, ZCUTS[k] % 128, ZCUTS[k + 1] - ZCUTS[k]
        to_z[k].wait_recv()
        go(to_diag[k])
        scale(far.at[half, c], lo, raw.at[1], ZCUTS[k], n)
        to_diag[k].wait_recv()
        scale(far.at[half, 1 - c], lo, raw.at[2], ZCUTS[k], n)

    def scale_e(k):
        half, lo, n = CUTS[k] // 128, CUTS[k] % 128, CUTS[k + 1] - CUTS[k]
        to_e[k].wait_recv()
        scale(ef.at[half], lo, rawe, CUTS[k], n)

    def near_own():
        for cc in range(2):
            p = nt(near[cc], near[c])
            for k in range(4):
                ps[0, k, cc] = p[128 * (k // 2):128 * (k // 2) + 128, 128 * (k % 2):128 * (k % 2) + 128]

    def near_ef(g, half):
        for cc in range(2):
            p = nt(near[cc], ef[half])
            for k in range(4):
                ps[g, k, cc] = p[128 * (k // 2):128 * (k // 2) + 128, 128 * (k % 2):128 * (k % 2) + 128]

    def far_with(g, slot, ra, right):
        p = nt(far[ra].reshape(256, rows), right)
        for cc in range(2):
            for k in range(2):
                ps[g, slot + k, cc] = p[128 * cc:128 * cc + 128, 128 * k:128 * k + 128]

    def sum_y_start(g):
        cs[g] = ps[g].astype(BF16)
        go(*sum_y[g])

    sum_y = [[remote(cs.at[g, (y + dy) % NY], rs.at[g, dy - 1], rs_s.at[g, dy - 1], rs_r.at[g, dy - 1],
                     at(l, (y + dy) % NY, h, x, c)) for dy in range(1, NY)] for g in range(EARLY)]
    sum_l = [remote(tmp.at[g, 1 - l], r2.at[g], r2_s.at[g], r2_r.at[g], at(1 - l, y, h, x, c)) for g in range(EARLY)]

    ring3 = [(dl, dy) for dl in range(2) for dy in range(NY) if (dl, dy) != (0, 0)]
    sum_s = {}
    for g in range(EARLY, SETS):
        sum_s[g] = [remote(cs.at[g, (y + dy) % NY, (l + dl) % 2], rd.at[g - EARLY, i], d_s.at[g - EARLY, i], d_r.at[g - EARLY, i],
                           at((l + dl) % 2, (y + dy) % NY, h, x, c)) for i, (dl, dy) in enumerate(ring3)]

    def sum_start(g):
        cs[g] = ps[g].astype(BF16)
        go(*sum_s[g])

    def total(g):
        if g < EARLY:
            sum_l[g].wait_recv()
            tot = tmp[g, l] + r2[g]
        else:
            for cp in sum_s[g]:
                cp.wait_recv()
            tot = ps[g, y, l]
            for i in range(len(ring3)):
                tot = tot + rd[g - EARLY, i].astype(F32)
        return tot * (1.0 / root)

    def sum_l_start(g):
        for cp in sum_y[g]:
            cp.wait_recv()
        tot = ps[g, y]
        for k in range(NY - 1):
            tot = tot + rs[g, k].astype(F32)
        tmp[g] = tot
        go(sum_l[g])

    def kinds(g):
        if g == 0:
            return [(None, False)]
        if g in MIXED:
            return [(y < 2, False), (y >= 2, True)]
        return [(None, True)]

    def under(cond, fn):
        if cond is None:
            fn()
        else:
            pl.when(cond)(fn)

    def asis(g, k, two):
        xd = (x + 3 - y % 2) % NX if two else x
        return remote(pc.at[g], fin.at[g, y, l], a_s.at[g, k], fin_r.at[g, l], at((l + k) % 2, y, h, xd, c))

    def turned(g, k):
        hd = (h + role(g, 3)[0]) % 2
        return remote(pt.at[g], fin.at[g, y, 2 + c], a_s.at[g, 2 + k], fin_r.at[g, 2 + c], at((l + k) % 2, y, hd, x, l))

    def publish(g):
        tot = total(g)
        pc[g] = tot.astype(BF16)
        if g > 0:
            pt[g] = tot.T.astype(BF16)
        for cond, two in kinds(g):
            def send(two=two):
                if two:
                    asis(g, 0, True).start()
                    asis(g, 1, True).start()
                    turned(g, 1).start()
                    if role(g, 3)[0]:
                        turned(g, 0).start()
                    else:
                        @pl.when(c == l)
                        def _():
                            pltpu.make_async_copy(pt.at[g], fin.at[g, y, 2 + c], fin_r.at[g, 2 + c]).start()

                        @pl.when(c != l)
                        def _():
                            turned(g, 0).start()
                else:
                    pltpu.make_async_copy(pc.at[g], fin.at[g, y, l], fin_r.at[g, l]).start()
                    asis(g, 1, False).start()
            under(cond, send)

    def along_y(g, dy, n):
        return remote(fin.at[g, y, pl.ds(0, n)], fin.at[g, y, pl.ds(0, n)], b_s.at[g, dy - 1], b_r.at[g, y],
                      at(l, (y + dy) % NY, h, x, c))

    def got(ref, sem):
        pltpu.make_async_copy(ref, ref, sem).wait()

    def spread(g):
        for cond, two in kinds(g):
            def send(two=two):
                n = 4 if two else 2
                for k in range(n):
                    got(fin.at[g, y, k], fin_r.at[g, k])
                for dy in range(1, NY):
                    along_y(g, dy, n).start()
            under(cond, send)

    def finish(g):
        for j in range(NY):
            n = 4 if role(g, j)[1] else 2

            @pl.when(y != j)
            def _():
                got(fin.at[g, j, pl.ds(0, n)], b_r.at[g, j])
        for cond, two in kinds(g):
            def wait(two=two):
                n = 4 if two else 2
                for dy in range(1, NY):
                    along_y(g, dy, n).wait_send()
                if two:
                    asis(g, 0, True).wait_send()
                    asis(g, 1, True).wait_send()
                    turned(g, 1).wait_send()
                    if role(g, 3)[0]:
                        turned(g, 0).wait_send()
                    else:
                        @pl.when(c != l)
                        def _():
                            turned(g, 0).wait_send()
                else:
                    asis(g, 1, False).wait_send()
            under(cond, wait)

    def asis_y(g, dy, two):
        xd = (x + 3 - y % 2) % NX if two else x
        return remote(pc.at[g], fin.at[g, y, l], ay_s.at[g, dy, 0], late_r.at[g, y, l], at(l, (y + dy) % NY, h, xd, c))

    def turned_y(g, dy):
        hd = (h + role(g, 3)[0]) % 2
        return remote(pt.at[g], fin.at[g, y, 2 + c], ay_s.at[g, dy, 1], late_r.at[g, y, 2 + c],
                      at(l, (y + dy) % NY, hd, x, l))

    def publish_late(g):
        tot = total(g)
        pc[g] = tot.astype(BF16)
        pt[g] = tot.T.astype(BF16)
        for cond, two in kinds(g):
            def send(two=two):
                for dy in range(1, NY):
                    asis_y(g, dy, two).start()
                    if two:
                        turned_y(g, dy).start()
                if two:
                    asis_y(g, 0, True).start()
                    if role(g, 3)[0]:
                        turned_y(g, 0).start()
                    else:
                        @pl.when(c == l)
                        def _():
                            pltpu.make_async_copy(pt.at[g], fin.at[g, y, 2 + c], late_r.at[g, y, 2 + c]).start()

                        @pl.when(c != l)
                        def _():
                            turned_y(g, 0).start()
                else:
                    pltpu.make_async_copy(pc.at[g], fin.at[g, y, l], late_r.at[g, y, l]).start()
            under(cond, send)

    def across_asis(g, j):
        return remote(fin.at[g, j, l], fin.at[g, j, l], al_s.at[g, j, 0], late_r.at[g, j, l], at(1 - l, y, h, x, c))

    def across_turned(g, j):
        pair = fin.at[g, j, pl.ds(2, 2)]
        return remote(pair, pair, al_s.at[g, j, 1], late_r.at[g, j, 2], at(1 - l, y, h, x, c))

    def spread_late(g):
        for j in range(NY):
            got(fin.at[g, j, l], late_r.at[g, j, l])
            across_asis(g, j).start()
        for j in range(NY):
            if role(g, j)[1]:
                @pl.when(c == l)
                def _():
                    for k in (2, 3):
                        got(fin.at[g, j, k], late_r.at[g, j, k])
                    across_turned(g, j).start()

    def finish_late(g):
        for j in range(NY):
            got(fin.at[g, j, 1 - l], late_r.at[g, j, 1 - l])
            across_asis(g, j).wait_send()
            if role(g, j)[1]:
                @pl.when(c != l)
                def _():
                    got(fin.at[g, j, pl.ds(2, 2)], late_r.at[g, j, 2])

                @pl.when(c == l)
                def _():
                    across_turned(g, j).wait_send()
        for cond, two in kinds(g):
            def wait(two=two):
                for dy in range(1, NY):
                    asis_y(g, dy, two).wait_send()
                    if two:
                        turned_y(g, dy).wait_send()
                if two:
                    asis_y(g, 0, True).wait_send()
                    if role(g, 3)[0]:
                        turned_y(g, 0).wait_send()
                    else:
                        @pl.when(c != l)
                        def _():
                            turned_y(g, 0).wait_send()
            under(cond, wait)

    scale(near.at[c], 0, xt, 0, cols)
    to_core.wait_recv()
    scale(near.at[1 - c], 0, raw.at[0], 0, cols)
    near_own()
    sum_y_start(0)
    redp[...] = nt(kept[...], near[c])
    dsend = []
    for i, (dl, dy) in enumerate(ring3):
        tl, ty = (l + dl) % 2, (y + dy) % NY
        dsend.append(remote(redp.at[pl.ds(pl.multiple_of((tl * NY + ty) * 8, 8), 8)], redr.at[i], rd_s.at[i], rd_r.at[i],
                            at(tl, ty, h, x, c)))
    go(*dsend)
    scale_e(0)
    scale_z(0)
    sum_l_start(0)
    scale_z(1)
    go(to_e[3], to_z[3])
    far_with(2, 0, 0, near[c])
    scale_e(1)
    for k in range(2):
        fwd[k].wait_recv()
        scale_f(k)
    near_ef(1, 0)
    sum_y_start(1)
    far_with(2, 2, 0, ef[0])
    sum_y_start(2)
    publish(0)
    to_f[2].wait_recv()
    go(fwd[2])
    scale_z(2)
    scale_e(2)
    sum_l_start(1)
    sum_l_start(2)
    go(to_e[4], to_z[4])
    to_f[3].wait_recv()
    go(fwd[3])
    scale_z(3)
    scale_e(3)
    spread(0)
    publish(1)
    publish(2)
    go(to_e[5], to_z[5])
    for k in (4, 5):
        to_f[k].wait_recv()
        go(fwd[k])
    for k in (2, 3):
        fwd[k].wait_recv()
        scale_f(k)
    scale_z(4)
    scale_e(4)
    spread(1)
    spread(2)
    scale_z(5)
    far_with(4, 2, 1, ef[0])
    far_with(5, 0, 1, near[c])
    scale_e(5)
    for k in (4, 5):
        fwd[k].wait_recv()
        scale_f(k)
    near_ef(3, 1)
    sum_start(3)
    far_with(4, 0, 0, ef[1])
    sum_start(4)
    far_with(5, 2, 1, ef[1])
    sum_start(5)
    publish_late(3)
    publish(4)
    spread_late(3)
    publish_late(5)
    spread(4)
    spread_late(5)
    for a in dsend:
        a.wait_recv()
    tot = redp[pl.ds(pl.multiple_of(s * 8, 8), 8), :]
    for i in range(len(ring3)):
        tot = tot + redr[i]
    red_ref[...] = tot
    for g in range(SETS):
        (finish_late if g in YFIRST else finish)(g)

    for cp in drain:
        cp.wait_send()


def assemble(place_ref, fin, red_in, gram_ref, red_ref):
    k = pl.program_id(0)
    h = place_ref[1]
    red_ref[...] = red_in[...]

    def tile(nf, block, row, col):
        return (h + nf) % 2, 0, pl.ds(block * 256 + row * 128, 128), pl.ds(col * 128, 128)

    for step in range(NX):
        @pl.when(k == step)
        def _():
            for g in range(SETS):
                for y in range(NY):
                    nf, kind, ra, cb = role(g, y)
                    if kind == step:
                        for j in range(2):
                            gram_ref[tile(nf, j, ra, cb)] = fin[g, y, j].astype(F32)
            for g in range(SETS):
                for y in range(NY):
                    nf, kind, ra, cb = role(g, y)
                    for j in range(2):
                        if kind == 1 and step == 3:
                            gram_ref[tile(nf, j, cb, ra)] = fin[g, y, 2 + j].astype(F32)
                        if kind == 2 and step == 2:
                            gram_ref[tile(nf, j, cb, ra)] += fin[g, y, 2 + j].astype(F32)


def local(snapshots, var_index, modes, retained):
    rows, cols = snapshots.shape
    n_space, n_time = lax.axis_size("space"), lax.axis_size("tm")
    total_rows = rows * n_space
    count = float(total_rows // VARS * (cols * n_time))
    root = float(total_rows) ** 0.5
    r = modes.shape[1]
    fk = (rows // 128 + 1) // 2 * 128
    dma = pltpu.SemaphoreType.DMA

    def body(*refs):
        kernel(count, root, fk, *refs)

    vmem = pl.BlockSpec(memory_space=pltpu.VMEM)
    nparts = len(CUTS) - 1
    fin, red = pl.pallas_call(
        body,
        name="gram",
        out_shape=(jax.ShapeDtypeStruct((SETS, NY, 4, 128, 128), BF16), jax.ShapeDtypeStruct((r // n_space, cols), F32)),
        in_specs=[vmem, vmem, vmem, pl.BlockSpec(memory_space=pltpu.SMEM)],
        out_specs=(pl.BlockSpec(memory_space=pl.ANY), vmem),
        scratch_shapes=[
            pltpu.VMEM((cols, rows), BF16),
            pltpu.VMEM((3, cols, rows), BF16),
            pltpu.VMEM((cols, rows), BF16),
            pltpu.VMEM((cols, fk), BF16),
            pltpu.VMEM((cols, fk), BF16),
            pltpu.VMEM((2, cols, rows), BF16),
            pltpu.VMEM((2, 2, 128, rows), BF16),
            pltpu.VMEM((2, 256, rows), BF16),
            pltpu.VMEM((VARS, rows), F32),
            pltpu.VMEM((1, rows), F32),
            pltpu.VMEM((1, rows), F32),
            pltpu.VMEM((r, rows), BF16),
            pltpu.VMEM((24, 128), F32),
            pltpu.VMEM((24, 128), F32),
            pltpu.VMEM((7, 24, 128), F32),
            pltpu.VMEM((15, 24, 128), F32),
            pltpu.VMEM((SETS, NY, 2, 128, 128), F32),
            pltpu.VMEM((SETS, NY, 2, 128, 128), BF16),
            pltpu.VMEM((EARLY, NY - 1, 2, 128, 128), BF16),
            pltpu.VMEM((EARLY, 2, 128, 128), F32),
            pltpu.VMEM((EARLY, 128, 128), F32),
            pltpu.VMEM((r, cols), F32),
            pltpu.VMEM((7, 8, cols), F32),
            pltpu.VMEM((SETS, 128, 128), BF16),
            pltpu.VMEM((SETS, 128, 128), BF16),
            dma((6, nparts)), dma((6, nparts)), dma((7,)), dma((7,)), dma((15,)), dma((15,)),
            dma((EARLY, 3)), dma((EARLY, 3)), dma((EARLY,)), dma((EARLY,)), dma((7,)), dma((7,)),
            dma((SETS, 4)), dma((SETS, 4)), dma((SETS, 3)), dma((SETS, NY)),
            dma((SETS, NY, 2)), dma((SETS, NY, 2)), dma((SETS, NY, 4)),
            pltpu.VMEM((SETS - EARLY, 7, 128, 128), BF16), dma((SETS - EARLY, 7)), dma((SETS - EARLY, 7)),
        ],
        compiler_params=pltpu.CompilerParams(
            collective_id=0, has_side_effects=True, vmem_limit_bytes=60 * 2 ** 20),
    )(snapshots, var_index, modes.T, retained)
    t = lax.axis_index("tm")
    spot = jnp.stack([(t // 2) % NX, t // 8])
    gram, red = pl.pallas_call(
        assemble,
        name="columns",
        grid_spec=pltpu.PrefetchScalarGridSpec(
            num_scalar_prefetch=1,
            grid=(NX,),
            in_specs=[pl.BlockSpec(fin.shape, lambda k, p: (0,) * 5), pl.BlockSpec(red.shape, lambda k, p: (0, 0))],
            out_specs=[pl.BlockSpec((2, 1, 2 * cols, cols), lambda k, p: (0, (p[0] + k) % NX, 0, 0)),
                       pl.BlockSpec(red.shape, lambda k, p: (0, 0))],
        ),
        out_shape=(jax.ShapeDtypeStruct((2, NX, 2 * cols, cols), F32), jax.ShapeDtypeStruct(red.shape, F32)),
        compiler_params=pltpu.CompilerParams(vmem_limit_bytes=60 * 2 ** 20),
    )(spot, fin, red)
    return gram.reshape(cols * n_time, cols), red


def solution(mesh):
    return jax.shard_map(
        local,
        mesh=mesh,
        in_specs=(P("space", "tm"), P("space"), P("space", None), P()),
        out_specs=(P(None, "tm"), P("space", "tm")),
        check_vma=False,
    )
```

```python
import jax
import jax.numpy as jnp
from jax import lax
from jax.experimental import pallas as pl
from jax.experimental.pallas import tpu as pltpu
from jax.sharding import PartitionSpec as P

MESH = pl.DeviceIdType.MESH
VARS = 8
NY, NX = 4, 4
F32, BF16 = jnp.float32, jnp.bfloat16


def place():
    s, t = lax.axis_index("space"), lax.axis_index("tm")
    return s // NY, s % NY, t // 8, (t // 2) % NX, t % 2


def at(l, y, h, x, c):
    return (l * NY + y, h * 8 + x * 2 + c)


def nt(a, b):
    return lax.dot_general(a, b, (((1,), (1,)), ((), ())), preferred_element_type=F32)


def pack(n, total, squares):
    lane = lax.broadcasted_iota(jnp.int32, (VARS, 128), 1)
    return jnp.where(lane == 0, n, jnp.where(lane == 1, total, squares))


def merge(tiles):
    n = sum(t[:, 0:1] for t in tiles)
    total = sum(t[:, 1:2] for t in tiles)
    mean = total / jnp.maximum(n, 1.0)
    squares = jnp.zeros_like(n)
    for t in tiles:
        off = t[:, 1:2] / jnp.maximum(t[:, 0:1], 1.0) - mean
        squares = squares + t[:, 2:3] + t[:, 0:1] * off * off
    return n, total, squares


def role(g, y):
    two, odd = y // 2, y % 2
    if g == 0:
        return 0, 0, two, odd
    if g in (1, 3):
        return 0, 1 + odd, two, g // 2
    if g == 4:
        return 1, 1 + odd, two, 1 - two
    last = g // 3
    return (1, 0, last, odd) if two == 0 else (1, 1 + odd, last, last)


SETS = 6
MIXED = (2, 5)
EARLY = 3
YFIRST = (3, 4)
CUTS = (0, 16, 64, 128, 160, 192, 224, 256)
ZCUTS = (0, 64, 128, 160, 192, 224, 256)


def kernel(count, root, fk, x_ref, vi_ref, modes_ref, ret_ref, fin, red_ref,
           xt, raw, rawe, relay, rawf, near, far, ef, hot, mean_l, inv_l, kept,
           tile1, tile2, got1, got2, ps, cs, rs, tmp, r2, redp, redr, pc, pt,
           bulk_s, bulk_r, st1_s, st1_r, st2_s, st2_r, rs_s, rs_r, r2_s, r2_r, rd_s, rd_r, a_s, fin_r, b_s, b_r,
           ay_s, al_s, late_r, rd, d_s, d_r):
    l, y, h, x, c = place()
    s = l * NY + y
    rows = xt.shape[1]
    cols = xt.shape[0]
    ntile = rows // 128
    drain = []

    ring1 = [(dx, dc) for dx in range(NX) for dc in range(2) if (dx, dc) != (0, 0)]
    ring2 = [(dy, dl, dh) for dy in range(NY) for dl in range(2) for dh in range(2) if (dy, dl, dh) != (0, 0, 0)]

    def dev1(dx, dc):
        return at(l, y, h, (x + dx) % NX, (c + dc) % 2)

    def dev2(dy, dl, dh):
        return at((l + dl) % 2, (y + dy) % NY, (h + dh) % 2, x, c)

    barrier = pltpu.get_barrier_semaphore()
    for d in ring1:
        pl.semaphore_signal(barrier, inc=1, device_id=dev1(*d), device_id_type=MESH)
    for d in ring2:
        pl.semaphore_signal(barrier, inc=1, device_id=dev2(*d), device_id_type=MESH)

    def turn(half):
        for k in range(ntile):
            xt[128 * half:128 * half + 128, 128 * k:128 * k + 128] = x_ref[128 * k:128 * k + 128, 128 * half:128 * half + 128].T

    turn(0)
    pl.semaphore_wait(barrier, len(ring1) + len(ring2))

    def remote(src, dst, ss, rsem, dev):
        return pltpu.make_async_remote_copy(src, dst, ss, rsem, device_id=dev, device_id_type=MESH)

    def go(*copies):
        for cp in copies:
            cp.start()
            drain.append(cp)

    fs_mine = pl.multiple_of((x // 2) * (rows - fk), 128)
    parts = [pl.ds(lo, hi - lo) for lo, hi in zip(CUTS, CUTS[1:])]
    to_f, to_e, to_z, to_core, to_diag, fwd = [], [], [], [], [], []
    left, core = at(l, y, h, (x + NX - 1) % NX, c), at(l, y, h, x, 1 - c)
    for k, r in enumerate(parts):
        to_f.append(remote(xt.at[r, pl.ds(fs_mine, fk)], relay.at[r], bulk_s.at[0, k], bulk_r.at[0, k], left))
        to_e.append(remote(xt.at[r], rawe.at[r], bulk_s.at[1, k], bulk_r.at[1, k], at(l, y, h, (x + 1) % NX, c)))
        fwd.append(remote(relay.at[r], rawf.at[r], bulk_s.at[5, k], bulk_r.at[5, k], left))
    for k, r in enumerate([pl.ds(lo, hi - lo) for lo, hi in zip(ZCUTS, ZCUTS[1:])]):
        to_z.append(remote(xt.at[r], raw.at[1, r], bulk_s.at[2, k], bulk_r.at[2, k], at(l, y, 1 - h, x, c)))
        to_diag.append(remote(raw.at[1, r], raw.at[2, r], bulk_s.at[4, k], bulk_r.at[4, k], core))
    to_core = remote(xt, raw.at[0], bulk_s.at[3, 0], bulk_r.at[3, 0], core)

    def pass_f(*ks):
        for k in ks:
            to_f[k].wait_recv()
            go(fwd[k])

    go(to_f[0], to_e[0], to_z[0])
    turn(1)
    go(to_core)

    hot[...] = (vi_ref[...][None, :] == lax.broadcasted_iota(jnp.int32, (VARS, rows), 0)).astype(F32)

    def colsum(fn):
        def body(k, acc):
            blk = xt[pl.ds(pl.multiple_of(k * 16, 16), 16), :].astype(F32)
            return acc + fn(blk)
        acc = lax.fori_loop(0, cols // 16, body, jnp.zeros((16, rows), F32))
        return jnp.sum(acc, axis=0, keepdims=True)

    n1 = jnp.sum(hot[...], axis=1, keepdims=True) * cols
    sum1 = jnp.sum(hot[...] * colsum(lambda b: b), axis=1, keepdims=True)
    m1 = sum1 / jnp.maximum(n1, 1.0)
    mean_l[...] = jnp.sum(hot[...] * m1, axis=0, keepdims=True)

    def sq(b):
        d = b - mean_l[...]
        return d * d
    sq1 = jnp.sum(hot[...] * colsum(sq), axis=1, keepdims=True)
    tile1[...] = pack(n1, sum1, sq1)
    sends1 = [remote(tile1, got1.at[i], st1_s.at[i], st1_r.at[i], dev1(*d)) for i, d in enumerate(ring1)]
    go(*sends1)
    go(to_f[1], to_e[1], to_f[2], to_e[2])
    keep = lax.broadcasted_iota(jnp.int32, kept.shape, 0) < ret_ref[0]
    kept[...] = jnp.where(keep, modes_ref[...].astype(F32), 0.0).astype(BF16)
    for half in range(2):
        ef[half, 128:256, :] = jnp.zeros((128, rows), BF16)
    for cp in sends1:
        cp.wait_recv()
    pass_f(0)
    n2, sum2, sq2 = merge([tile1[...]] + [got1[i] for i in range(len(ring1))])
    tile2[...] = pack(n2, sum2, sq2)
    sends2 = [remote(tile2, got2.at[i], st2_s.at[i], st2_r.at[i], dev2(*d)) for i, d in enumerate(ring2)]
    go(*sends2)
    go(to_z[1])
    pass_f(1)
    for cp in sends2:
        cp.wait_recv()
    _, sum3, sq3 = merge([tile2[...]] + [got2[i] for i in range(len(ring2))])
    mean = sum3 / count
    inv = 1.0 / jnp.sqrt(sq3 / count + 1e-06)
    mean_l[...] = jnp.sum(hot[...] * mean, axis=0, keepdims=True)
    inv_l[...] = jnp.sum(hot[...] * inv, axis=0, keepdims=True)
    go(to_z[2])

    def scale_to(dst, dlo, src, lo, n, m, v):
        def body(k, _):
            a = pl.multiple_of(k * 16, 16)
            dst[pl.ds(dlo + a, 16), :] = ((src[pl.ds(lo + a, 16), :].astype(F32) - m) * v).astype(BF16)
            return 0
        lax.fori_loop(0, n // 16, body, 0)

    def scale(dst, dlo, src, lo, n):
        scale_to(dst, dlo, src, lo, n, mean_l[...], inv_l[...])

    fs = pl.multiple_of((((x + 2) % NX) // 2) * (rows - fk), 128)
    fl = pl.ds(fs, fk)
    over = 2 * fk - rows
    first = lax.broadcasted_iota(jnp.int32, (1, fk), 1) < over
    drop = jnp.logical_and(first, x < 2)

    def scale_f(k):
        half, lo = CUTS[k] // 128, CUTS[k] % 128
        scale_to(ef.at[half, :, fl], 128 + lo, rawf, CUTS[k], CUTS[k + 1] - CUTS[k], mean_l[:, fl],
                 jnp.where(drop, 0.0, inv_l[:, fl]))

    def pass_z(k):
        to_z[k].wait_recv()
        go(to_diag[k])

    def scale_z(k):
        half, lo, n = ZCUTS[k] // 128, ZCUTS[k] % 128, ZCUTS[k + 1] - ZCUTS[k]
        scale(far.at[half, c], lo, raw.at[1], ZCUTS[k], n)
        to_diag[k].wait_recv()
        scale(far.at[half, 1 - c], lo, raw.at[2], ZCUTS[k], n)

    def take_f(*ks):
        for k in ks:
            fwd[k].wait_recv()
            scale_f(k)

    def scale_e(k):
        half, lo, n = CUTS[k] // 128, CUTS[k] % 128, CUTS[k + 1] - CUTS[k]
        to_e[k].wait_recv()
        scale(ef.at[half], lo, rawe, CUTS[k], n)

    def near_own():
        for cc in range(2):
            p = nt(near[cc], near[c])
            for k in range(4):
                ps[0, k, cc] = p[128 * (k // 2):128 * (k // 2) + 128, 128 * (k % 2):128 * (k % 2) + 128]

    def near_ef(g, half):
        for cc in range(2):
            p = nt(near[cc], ef[half])
            for k in range(4):
                ps[g, k, cc] = p[128 * (k // 2):128 * (k // 2) + 128, 128 * (k % 2):128 * (k % 2) + 128]

    def far_with(g, slot, ra, right):
        p = nt(far[ra].reshape(256, rows), right)
        for cc in range(2):
            for k in range(2):
                ps[g, slot + k, cc] = p[128 * cc:128 * cc + 128, 128 * k:128 * k + 128]

    def sum_y_start(g):
        cs[g] = ps[g].astype(BF16)
        go(*sum_y[g])

    sum_y = [[remote(cs.at[g, (y + dy) % NY], rs.at[g, dy - 1], rs_s.at[g, dy - 1], rs_r.at[g, dy - 1],
                     at(l, (y + dy) % NY, h, x, c)) for dy in range(1, NY)] for g in range(EARLY)]
    sum_l = [remote(tmp.at[g, 1 - l], r2.at[g], r2_s.at[g], r2_r.at[g], at(1 - l, y, h, x, c)) for g in range(EARLY)]

    ring3 = [(dl, dy) for dl in range(2) for dy in range(NY) if (dl, dy) != (0, 0)]
    sum_s = {}
    for g in range(EARLY, SETS):
        sum_s[g] = [remote(cs.at[g, (y + dy) % NY, (l + dl) % 2], rd.at[g - EARLY, i], d_s.at[g - EARLY, i], d_r.at[g - EARLY, i],
                           at((l + dl) % 2, (y + dy) % NY, h, x, c)) for i, (dl, dy) in enumerate(ring3)]

    def sum_start(g):
        cs[g] = ps[g].astype(BF16)
        go(*sum_s[g])

    def total(g):
        if g < EARLY:
            sum_l[g].wait_recv()
            tot = tmp[g, l] + r2[g]
        else:
            for cp in sum_s[g]:
                cp.wait_recv()
            tot = ps[g, y, l]
            for i in range(len(ring3)):
                tot = tot + rd[g - EARLY, i].astype(F32)
        return tot * (1.0 / root)

    def sum_l_start(g):
        for cp in sum_y[g]:
            cp.wait_recv()
        tot = ps[g, y]
        for k in range(NY - 1):
            tot = tot + rs[g, k].astype(F32)
        tmp[g] = tot
        go(sum_l[g])

    def kinds(g):
        if g == 0:
            return [(None, False)]
        if g in MIXED:
            return [(y < 2, False), (y >= 2, True)]
        return [(None, True)]

    def under(cond, fn):
        if cond is None:
            fn()
        else:
            pl.when(cond)(fn)

    def asis(g, k, two):
        xd = (x + 3 - y % 2) % NX if two else x
        return remote(pc.at[g], fin.at[g, y, l], a_s.at[g, k], fin_r.at[g, l], at((l + k) % 2, y, h, xd, c))

    def turned(g, k):
        hd = (h + role(g, 3)[0]) % 2
        return remote(pt.at[g], fin.at[g, y, 2 + c], a_s.at[g, 2 + k], fin_r.at[g, 2 + c], at((l + k) % 2, y, hd, x, l))

    def publish(g):
        tot = total(g)
        pc[g] = tot.astype(BF16)
        if g > 0:
            pt[g] = tot.T.astype(BF16)
        for cond, two in kinds(g):
            def send(two=two):
                if two:
                    asis(g, 0, True).start()
                    asis(g, 1, True).start()
                    turned(g, 1).start()
                    if role(g, 3)[0]:
                        turned(g, 0).start()
                    else:
                        @pl.when(c == l)
                        def _():
                            pltpu.make_async_copy(pt.at[g], fin.at[g, y, 2 + c], fin_r.at[g, 2 + c]).start()

                        @pl.when(c != l)
                        def _():
                            turned(g, 0).start()
                else:
                    pltpu.make_async_copy(pc.at[g], fin.at[g, y, l], fin_r.at[g, l]).start()
                    asis(g, 1, False).start()
            under(cond, send)

    def along_y(g, dy, n):
        return remote(fin.at[g, y, pl.ds(0, n)], fin.at[g, y, pl.ds(0, n)], b_s.at[g, dy - 1], b_r.at[g, y],
                      at(l, (y + dy) % NY, h, x, c))

    def got(ref, sem):
        pltpu.make_async_copy(ref, ref, sem).wait()

    def spread(g):
        for cond, two in kinds(g):
            def send(two=two):
                n = 4 if two else 2
                for k in range(n):
                    got(fin.at[g, y, k], fin_r.at[g, k])
                for dy in range(1, NY):
                    along_y(g, dy, n).start()
            under(cond, send)

    def finish(g):
        for j in range(NY):
            n = 4 if role(g, j)[1] else 2

            @pl.when(y != j)
            def _():
                got(fin.at[g, j, pl.ds(0, n)], b_r.at[g, j])
        for cond, two in kinds(g):
            def wait(two=two):
                n = 4 if two else 2
                for dy in range(1, NY):
                    along_y(g, dy, n).wait_send()
                if two:
                    asis(g, 0, True).wait_send()
                    asis(g, 1, True).wait_send()
                    turned(g, 1).wait_send()
                    if role(g, 3)[0]:
                        turned(g, 0).wait_send()
                    else:
                        @pl.when(c != l)
                        def _():
                            turned(g, 0).wait_send()
                else:
                    asis(g, 1, False).wait_send()
            under(cond, wait)

    def asis_y(g, dy, two):
        xd = (x + 3 - y % 2) % NX if two else x
        return remote(pc.at[g], fin.at[g, y, l], ay_s.at[g, dy, 0], late_r.at[g, y, l], at(l, (y + dy) % NY, h, xd, c))

    def turned_y(g, dy):
        hd = (h + role(g, 3)[0]) % 2
        return remote(pt.at[g], fin.at[g, y, 2 + c], ay_s.at[g, dy, 1], late_r.at[g, y, 2 + c],
                      at(l, (y + dy) % NY, hd, x, l))

    def publish_late(g):
        tot = total(g)
        pc[g] = tot.astype(BF16)
        pt[g] = tot.T.astype(BF16)
        for cond, two in kinds(g):
            def send(two=two):
                for dy in range(1, NY):
                    asis_y(g, dy, two).start()
                    if two:
                        turned_y(g, dy).start()
                if two:
                    asis_y(g, 0, True).start()
                    if role(g, 3)[0]:
                        turned_y(g, 0).start()
                    else:
                        @pl.when(c == l)
                        def _():
                            pltpu.make_async_copy(pt.at[g], fin.at[g, y, 2 + c], late_r.at[g, y, 2 + c]).start()

                        @pl.when(c != l)
                        def _():
                            turned_y(g, 0).start()
                else:
                    pltpu.make_async_copy(pc.at[g], fin.at[g, y, l], late_r.at[g, y, l]).start()
            under(cond, send)

    def across_asis(g, j):
        return remote(fin.at[g, j, l], fin.at[g, j, l], al_s.at[g, j, 0], late_r.at[g, j, l], at(1 - l, y, h, x, c))

    def across_turned(g, j):
        pair = fin.at[g, j, pl.ds(2, 2)]
        return remote(pair, pair, al_s.at[g, j, 1], late_r.at[g, j, 2], at(1 - l, y, h, x, c))

    def spread_late(g):
        for j in range(NY):
            got(fin.at[g, j, l], late_r.at[g, j, l])
            across_asis(g, j).start()
        for j in range(NY):
            if role(g, j)[1]:
                @pl.when(c == l)
                def _():
                    for k in (2, 3):
                        got(fin.at[g, j, k], late_r.at[g, j, k])
                    across_turned(g, j).start()

    def finish_late(g):
        for j in range(NY):
            got(fin.at[g, j, 1 - l], late_r.at[g, j, 1 - l])
            across_asis(g, j).wait_send()
            if role(g, j)[1]:
                @pl.when(c != l)
                def _():
                    got(fin.at[g, j, pl.ds(2, 2)], late_r.at[g, j, 2])

                @pl.when(c == l)
                def _():
                    across_turned(g, j).wait_send()
        for cond, two in kinds(g):
            def wait(two=two):
                for dy in range(1, NY):
                    asis_y(g, dy, two).wait_send()
                    if two:
                        turned_y(g, dy).wait_send()
                if two:
                    asis_y(g, 0, True).wait_send()
                    if role(g, 3)[0]:
                        turned_y(g, 0).wait_send()
                    else:
                        @pl.when(c != l)
                        def _():
                            turned_y(g, 0).wait_send()
            under(cond, wait)

    pass_f(2)
    go(to_e[3], to_e[4], *to_f[3:])
    scale(near.at[c], 0, xt, 0, cols)
    pass_z(0)
    to_core.wait_recv()
    scale(near.at[1 - c], 0, raw.at[0], 0, cols)
    near_own()
    sum_y_start(0)
    redp[...] = nt(kept[...], near[c])
    dsend = []
    for i, (dl, dy) in enumerate(ring3):
        tl, ty = (l + dl) % 2, (y + dy) % NY
        dsend.append(remote(redp.at[pl.ds(pl.multiple_of((tl * NY + ty) * 8, 8), 8)], redr.at[i], rd_s.at[i], rd_r.at[i],
                            at(tl, ty, h, x, c)))
    go(*dsend)
    scale_e(0)
    scale_e(1)
    scale_z(0)
    pass_z(1)
    sum_l_start(0)
    go(to_z[3], to_e[5], to_e[6])
    scale_e(2)
    take_f(0, 1, 2)
    near_ef(1, 0)
    sum_y_start(1)
    scale_z(1)
    far_with(2, 0, 0, near[c])
    far_with(2, 2, 0, ef[0])
    sum_y_start(2)
    publish(0)
    go(to_z[4])
    pass_f(3)
    pass_z(2)
    scale_e(3)
    scale_z(2)
    pass_f(4)
    sum_l_start(1)
    pass_z(3)
    pass_f(5)
    scale_z(3)
    sum_l_start(2)
    go(to_z[5])
    pass_f(6)
    scale_e(4)
    spread(0)
    take_f(3, 4)
    publish(1)
    publish(2)
    scale_e(5)
    scale_e(6)
    pass_z(4)
    take_f(5, 6)
    near_ef(3, 1)
    sum_start(3)
    scale_z(4)
    far_with(4, 0, 0, ef[1])
    pass_z(5)
    spread(1)
    scale_z(5)
    far_with(4, 2, 1, ef[0])
    sum_start(4)
    far_with(5, 0, 1, near[c])
    far_with(5, 2, 1, ef[1])
    sum_start(5)
    publish_late(3)
    publish_late(4)
    spread(2)
    publish(5)
    spread_late(3)
    spread_late(4)
    spread(5)
    for a in dsend:
        a.wait_recv()
    tot = redp[pl.ds(pl.multiple_of(s * 8, 8), 8), :]
    for i in range(len(ring3)):
        tot = tot + redr[i]
    red_ref[...] = tot
    for g in range(SETS):
        (finish_late if g in YFIRST else finish)(g)

    for cp in drain:
        cp.wait_send()


def assemble(fin, red_in, gram, red_ref, held, block, in_sem, out_sem):
    _, _, h, x, _ = place()
    loads = [pltpu.make_async_copy(fin.at[g], held.at[g], in_sem.at[g]) for g in range(SETS)]
    for cp in loads:
        cp.start()
    red_ref[...] = red_in[...]

    def tile(step, nf, half, row, col):
        return step, (h + nf) % 2, pl.ds(half * 256 + row * 128, 128), pl.ds(col * 128, 128)

    for cp in loads:
        cp.wait()
    for step in (0, 1, 3, 2):
        for g in range(SETS):
            for y in range(NY):
                nf, kind, ra, cb = role(g, y)
                for j in range(2):
                    if kind == step:
                        block[tile(step, nf, j, ra, cb)] = held[g, y, j].astype(F32)
                    if kind == 1 and step == 3:
                        block[tile(step, nf, j, cb, ra)] = held[g, y, 2 + j].astype(F32)
        if step == 2:
            for g in range(SETS):
                for y in range(NY):
                    nf, kind, ra, cb = role(g, y)
                    if kind == 2:
                        for j in range(2):
                            block[tile(step, nf, j, cb, ra)] += held[g, y, 2 + j].astype(F32)
        pltpu.make_async_copy(block.at[step], gram.at[:, (x + step) % NX], out_sem.at[step]).start()
    for step in range(NX):
        pltpu.make_async_copy(block.at[step], gram.at[:, (x + step) % NX], out_sem.at[step]).wait()


def local(snapshots, var_index, modes, retained):
    rows, cols = snapshots.shape
    n_space, n_time = lax.axis_size("space"), lax.axis_size("tm")
    total_rows = rows * n_space
    count = float(total_rows // VARS * (cols * n_time))
    root = float(total_rows) ** 0.5
    r = modes.shape[1]
    fk = (rows // 128 + 1) // 2 * 128
    dma = pltpu.SemaphoreType.DMA

    def body(*refs):
        kernel(count, root, fk, *refs)

    vmem = pl.BlockSpec(memory_space=pltpu.VMEM)
    nparts = len(CUTS) - 1
    fin, red = pl.pallas_call(
        body,
        name="gram",
        out_shape=(jax.ShapeDtypeStruct((SETS, NY, 4, 128, 128), BF16), jax.ShapeDtypeStruct((r // n_space, cols), F32)),
        in_specs=[vmem, vmem, vmem, pl.BlockSpec(memory_space=pltpu.SMEM)],
        out_specs=(pl.BlockSpec(memory_space=pl.ANY), vmem),
        scratch_shapes=[
            pltpu.VMEM((cols, rows), BF16),
            pltpu.VMEM((3, cols, rows), BF16),
            pltpu.VMEM((cols, rows), BF16),
            pltpu.VMEM((cols, fk), BF16),
            pltpu.VMEM((cols, fk), BF16),
            pltpu.VMEM((2, cols, rows), BF16),
            pltpu.VMEM((2, 2, 128, rows), BF16),
            pltpu.VMEM((2, 256, rows), BF16),
            pltpu.VMEM((VARS, rows), F32),
            pltpu.VMEM((1, rows), F32),
            pltpu.VMEM((1, rows), F32),
            pltpu.VMEM((r, rows), BF16),
            pltpu.VMEM((VARS, 128), F32),
            pltpu.VMEM((VARS, 128), F32),
            pltpu.VMEM((7, VARS, 128), F32),
            pltpu.VMEM((15, VARS, 128), F32),
            pltpu.VMEM((SETS, NY, 2, 128, 128), F32),
            pltpu.VMEM((SETS, NY, 2, 128, 128), BF16),
            pltpu.VMEM((EARLY, NY - 1, 2, 128, 128), BF16),
            pltpu.VMEM((EARLY, 2, 128, 128), F32),
            pltpu.VMEM((EARLY, 128, 128), F32),
            pltpu.VMEM((r, cols), F32),
            pltpu.VMEM((7, 8, cols), F32),
            pltpu.VMEM((SETS, 128, 128), BF16),
            pltpu.VMEM((SETS, 128, 128), BF16),
            dma((6, nparts)), dma((6, nparts)), dma((7,)), dma((7,)), dma((15,)), dma((15,)),
            dma((EARLY, 3)), dma((EARLY, 3)), dma((EARLY,)), dma((EARLY,)), dma((7,)), dma((7,)),
            dma((SETS, 4)), dma((SETS, 4)), dma((SETS, 3)), dma((SETS, NY)),
            dma((SETS, NY, 2)), dma((SETS, NY, 2)), dma((SETS, NY, 4)),
            pltpu.VMEM((SETS - EARLY, 7, 128, 128), BF16), dma((SETS - EARLY, 7)), dma((SETS - EARLY, 7)),
        ],
        compiler_params=pltpu.CompilerParams(
            collective_id=0, has_side_effects=True, vmem_limit_bytes=60 * 2 ** 20),
    )(snapshots, var_index, modes.T, retained)
    gram, red = pl.pallas_call(
        assemble,
        name="columns",
        in_specs=[pl.BlockSpec(memory_space=pl.ANY), vmem],
        out_specs=(pl.BlockSpec(memory_space=pl.ANY), vmem),
        out_shape=(jax.ShapeDtypeStruct((2, NX, 2 * cols, cols), F32), jax.ShapeDtypeStruct(red.shape, F32)),
        scratch_shapes=[pltpu.VMEM(fin.shape, BF16), pltpu.VMEM((NX, 2, 2 * cols, cols), F32), dma((SETS,)), dma((NX,))],
        compiler_params=pltpu.CompilerParams(vmem_limit_bytes=60 * 2 ** 20),
    )(fin, red)
    return gram.reshape(cols * n_time, cols), red


def solution(mesh):
    return jax.shard_map(
        local,
        mesh=mesh,
        in_specs=(P("space", "tm"), P("space"), P("space", None), P()),
        out_specs=(P(None, "tm"), P("space", "tm")),
        check_vma=False,
    )
```

```python
import jax
import jax.numpy as jnp
from jax import lax
from jax.experimental import pallas as pl
from jax.experimental.pallas import tpu as pltpu
from jax.sharding import PartitionSpec as P

MESH = pl.DeviceIdType.MESH
VARS = 8
NY, NX = 4, 4
F32, BF16 = jnp.float32, jnp.bfloat16


def place():
    s, t = lax.axis_index("space"), lax.axis_index("tm")
    return s // NY, s % NY, t // 8, (t // 2) % NX, t % 2


def at(l, y, h, x, c):
    return (l * NY + y, h * 8 + x * 2 + c)


def nt(a, b):
    return lax.dot_general(a, b, (((1,), (1,)), ((), ())), preferred_element_type=F32)


def pack(n, total, squares):
    lane = lax.broadcasted_iota(jnp.int32, (VARS, 128), 1)
    return jnp.where(lane == 0, n, jnp.where(lane == 1, total, squares))


def merge(tiles):
    n = sum(t[:, 0:1] for t in tiles)
    total = sum(t[:, 1:2] for t in tiles)
    mean = total / jnp.maximum(n, 1.0)
    squares = jnp.zeros_like(n)
    for t in tiles:
        off = t[:, 1:2] / jnp.maximum(t[:, 0:1], 1.0) - mean
        squares = squares + t[:, 2:3] + t[:, 0:1] * off * off
    return n, total, squares


def role(g, y):
    two, odd = y // 2, y % 2
    if g == 0:
        return 0, 0, two, odd
    if g in (1, 3):
        return 0, 1 + odd, two, g // 2
    if g == 4:
        return 1, 1 + odd, two, 1 - two
    last = g // 3
    return (1, 0, last, odd) if two == 0 else (1, 1 + odd, last, last)


SETS = 6
MIXED = (2, 5)
EARLY = 3
YFIRST = (1, 2, 5)
ZFIRST = (0, 3, 4)
CUTS = (0, 16, 64, 128, 160, 192, 224, 256)
ZCUTS = (0, 64, 128, 160, 192, 224, 256)


def kernel(count, root, fk, x_ref, vi_ref, modes_ref, ret_ref, fin, red_ref,
           xt, raw, rawe, relay, rawf, near, far, ef, hot, mean_l, inv_l, kept,
           tile1, tile2, got1, got2, ps, cs, rs, tmp, r2, redp, redr, pc, pt,
           rd, bulk_s, bulk_r, st_s, st_r, rs_s, rs_r, r2_s, r2_r, d_s, d_r, zf_s, zf_r, yf_s, yf_r):
    l, y, h, x, c = place()
    s = l * NY + y
    rows = xt.shape[1]
    cols = xt.shape[0]
    ntile = rows // 128

    ring1 = [(dx, dc) for dx in range(NX) for dc in range(2) if (dx, dc) != (0, 0)]
    ring2 = [(dy, dl, dh) for dy in range(NY) for dl in range(2) for dh in range(2) if (dy, dl, dh) != (0, 0, 0)]

    def dev1(dx, dc):
        return at(l, y, h, (x + dx) % NX, (c + dc) % 2)

    def dev2(dy, dl, dh):
        return at((l + dl) % 2, (y + dy) % NY, (h + dh) % 2, x, c)

    barrier = pltpu.get_barrier_semaphore()
    for d in ring1:
        pl.semaphore_signal(barrier, inc=1, device_id=dev1(*d), device_id_type=MESH)
    for d in ring2:
        pl.semaphore_signal(barrier, inc=1, device_id=dev2(*d), device_id_type=MESH)

    def turn(half):
        for k in range(ntile):
            xt[128 * half:128 * half + 128, 128 * k:128 * k + 128] = x_ref[128 * k:128 * k + 128, 128 * half:128 * half + 128].T

    turn(0)
    pl.semaphore_wait(barrier, len(ring1) + len(ring2))

    def remote(src, dst, ss, rsem, dev):
        return pltpu.make_async_remote_copy(src, dst, ss, rsem, device_id=dev, device_id_type=MESH)

    def go(*copies):
        for cp in copies:
            cp.start()

    def got(ref, sem):
        pltpu.make_async_copy(ref, ref, sem).wait()

    fs_mine = pl.multiple_of((x // 2) * (rows - fk), 128)
    parts = [pl.ds(lo, hi - lo) for lo, hi in zip(CUTS, CUTS[1:])]
    to_f, to_e, to_z, to_core, to_diag, fwd = [], [], [], [], [], []
    left, core = at(l, y, h, (x + NX - 1) % NX, c), at(l, y, h, x, 1 - c)
    nf, nz = len(CUTS) - 1, len(ZCUTS) - 1
    for k, r in enumerate(parts):
        to_f.append(remote(xt.at[r, pl.ds(fs_mine, fk)], relay.at[r], bulk_s.at[0], bulk_r.at[k], left))
        to_e.append(remote(xt.at[r], rawe.at[r], bulk_s.at[1], bulk_r.at[nf + k], at(l, y, h, (x + 1) % NX, c)))
        fwd.append(remote(relay.at[r], rawf.at[r], bulk_s.at[5], bulk_r.at[2 * nf + k], left))
    for k, r in enumerate([pl.ds(lo, hi - lo) for lo, hi in zip(ZCUTS, ZCUTS[1:])]):
        to_z.append(remote(xt.at[r], raw.at[1, r], bulk_s.at[2], bulk_r.at[3 * nf + k], at(l, y, 1 - h, x, c)))
        to_diag.append(remote(raw.at[1, r], raw.at[2, r], bulk_s.at[4], bulk_r.at[3 * nf + nz + k], core))
    to_core = remote(xt, raw.at[0], bulk_s.at[3], bulk_r.at[3 * nf + 2 * nz], core)

    def pass_f(*ks):
        for k in ks:
            to_f[k].wait_recv()
            go(fwd[k])

    go(to_f[0], to_e[0], to_z[0])
    turn(1)
    go(to_core)

    hot[...] = (vi_ref[...][None, :] == lax.broadcasted_iota(jnp.int32, (VARS, rows), 0)).astype(F32)

    def colsum(fn):
        def body(k, acc):
            blk = xt[pl.ds(pl.multiple_of(k * 16, 16), 16), :].astype(F32)
            return acc + fn(blk)
        acc = lax.fori_loop(0, cols // 16, body, jnp.zeros((16, rows), F32))
        return jnp.sum(acc, axis=0, keepdims=True)

    n1 = jnp.sum(hot[...], axis=1, keepdims=True) * cols
    sum1 = jnp.sum(hot[...] * colsum(lambda b: b), axis=1, keepdims=True)
    m1 = sum1 / jnp.maximum(n1, 1.0)
    mean_l[...] = jnp.sum(hot[...] * m1, axis=0, keepdims=True)

    def sq(b):
        d = b - mean_l[...]
        return d * d
    sq1 = jnp.sum(hot[...] * colsum(sq), axis=1, keepdims=True)
    tile1[...] = pack(n1, sum1, sq1)
    sends1 = [remote(tile1, got1.at[i], st_s.at[0], st_r.at[0], dev1(*d)) for i, d in enumerate(ring1)]
    go(*sends1)
    go(to_f[1], to_e[1], to_f[2], to_e[2])
    keep = lax.broadcasted_iota(jnp.int32, kept.shape, 0) < ret_ref[0]
    kept[...] = jnp.where(keep, modes_ref[...].astype(F32), 0.0).astype(BF16)
    for half in range(2):
        ef[half, 128:256, :] = jnp.zeros((128, rows), BF16)
    got(got1, st_r.at[0])
    pass_f(0)
    n2, sum2, sq2 = merge([tile1[...]] + [got1[i] for i in range(len(ring1))])
    tile2[...] = pack(n2, sum2, sq2)
    sends2 = [remote(tile2, got2.at[i], st_s.at[1], st_r.at[1], dev2(*d)) for i, d in enumerate(ring2)]
    go(*sends2)
    go(to_z[1])
    pass_f(1)
    got(got2, st_r.at[1])
    _, sum3, sq3 = merge([tile2[...]] + [got2[i] for i in range(len(ring2))])
    mean = sum3 / count
    inv = 1.0 / jnp.sqrt(sq3 / count + 1e-06)
    mean_l[...] = jnp.sum(hot[...] * mean, axis=0, keepdims=True)
    inv_l[...] = jnp.sum(hot[...] * inv, axis=0, keepdims=True)
    go(to_z[2])

    def scale_to(dst, dlo, src, lo, n, m, v):
        def body(k, _):
            a = pl.multiple_of(k * 16, 16)
            dst[pl.ds(dlo + a, 16), :] = ((src[pl.ds(lo + a, 16), :].astype(F32) - m) * v).astype(BF16)
            return 0
        lax.fori_loop(0, n // 16, body, 0)

    def scale(dst, dlo, src, lo, n):
        scale_to(dst, dlo, src, lo, n, mean_l[...], inv_l[...])

    fs = pl.multiple_of((((x + 2) % NX) // 2) * (rows - fk), 128)
    fl = pl.ds(fs, fk)
    over = 2 * fk - rows
    first = lax.broadcasted_iota(jnp.int32, (1, fk), 1) < over
    drop = jnp.logical_and(first, x < 2)

    def scale_f(k):
        half, lo = CUTS[k] // 128, CUTS[k] % 128
        scale_to(ef.at[half, :, fl], 128 + lo, rawf, CUTS[k], CUTS[k + 1] - CUTS[k], mean_l[:, fl],
                 jnp.where(drop, 0.0, inv_l[:, fl]))

    def pass_z(k):
        to_z[k].wait_recv()
        go(to_diag[k])

    def scale_z(k):
        half, lo, n = ZCUTS[k] // 128, ZCUTS[k] % 128, ZCUTS[k + 1] - ZCUTS[k]
        scale(far.at[half, c], lo, raw.at[1], ZCUTS[k], n)
        to_diag[k].wait_recv()
        scale(far.at[half, 1 - c], lo, raw.at[2], ZCUTS[k], n)

    def take_f(*ks):
        for k in ks:
            fwd[k].wait_recv()
            scale_f(k)

    def scale_e(k):
        half, lo, n = CUTS[k] // 128, CUTS[k] % 128, CUTS[k + 1] - CUTS[k]
        to_e[k].wait_recv()
        scale(ef.at[half], lo, rawe, CUTS[k], n)

    def near_own():
        for cc in range(2):
            p = nt(near[cc], near[c])
            for k in range(4):
                ps[0, k, cc] = p[128 * (k // 2):128 * (k // 2) + 128, 128 * (k % 2):128 * (k % 2) + 128]

    def near_ef(g, half):
        for cc in range(2):
            p = nt(near[cc], ef[half])
            for k in range(4):
                ps[g, k, cc] = p[128 * (k // 2):128 * (k // 2) + 128, 128 * (k % 2):128 * (k % 2) + 128]

    def far_with(g, slot, ra, right):
        p = nt(far[ra].reshape(256, rows), right)
        for cc in range(2):
            for k in range(2):
                ps[g, slot + k, cc] = p[128 * cc:128 * cc + 128, 128 * k:128 * k + 128]

    def sum_y_start(g):
        cs[g] = ps[g].astype(BF16)
        go(*sum_y[g])

    sum_y = [[remote(cs.at[g, (y + dy) % NY], rs.at[g, dy - 1], rs_s.at[g], rs_r.at[g],
                     at(l, (y + dy) % NY, h, x, c)) for dy in range(1, NY)] for g in range(EARLY)]
    sum_l = [remote(tmp.at[g, 1 - l], r2.at[g], r2_s.at[g], r2_r.at[g], at(1 - l, y, h, x, c)) for g in range(EARLY)]

    ring3 = [(dl, dy) for dl in range(2) for dy in range(NY) if (dl, dy) != (0, 0)]
    sum_s = {}
    for g in range(EARLY, SETS):
        sum_s[g] = [remote(cs.at[g, (y + dy) % NY, (l + dl) % 2], rd.at[g - EARLY, i], d_s.at[g - EARLY], d_r.at[g - EARLY],
                           at((l + dl) % 2, (y + dy) % NY, h, x, c)) for i, (dl, dy) in enumerate(ring3)]

    def sum_start(g):
        cs[g] = ps[g].astype(BF16)
        go(*sum_s[g])

    def total(g):
        if g < EARLY:
            sum_l[g].wait_recv()
            tot = tmp[g, l] + r2[g]
        else:
            got(rd.at[g - EARLY], d_r.at[g - EARLY])
            tot = ps[g, y, l]
            for i in range(len(ring3)):
                tot = tot + rd[g - EARLY, i].astype(F32)
        return tot * (1.0 / root)

    def sum_l_start(g):
        got(rs.at[g], rs_r.at[g])
        tot = ps[g, y]
        for k in range(NY - 1):
            tot = tot + rs[g, k].astype(F32)
        tmp[g] = tot
        go(sum_l[g])

    def kinds(g):
        if g == 0:
            return [(None, False)]
        if g in MIXED:
            return [(y < 2, False), (y >= 2, True)]
        return [(None, True)]

    def under(cond, fn):
        if cond is None:
            fn()
        else:
            pl.when(cond)(fn)

    def slots(n):
        return cs.at[0] if n == 8 else rd.at[0, pl.ds(0, n)]

    def publish(g):
        zf = g in ZFIRST
        i = (ZFIRST if zf else YFIRST).index(g)
        send, cond_send = (zf_s.at[i, 0], zf_s.at[i, 1]) if zf else (yf_s.at[i, 0], yf_s.at[i, 1])
        recv, recv_t = (zf_r.at[i, 0], zf_r.at[i, 0]) if zf else (yf_r.at[i, 0], yf_r.at[i, 1])
        far_set = role(g, 3)[0]
        spots = [((l + k) % 2, y) for k in range(2)] if zf else [(l, (y + k) % NY) for k in range(NY)]
        tot = total(g)
        pc[g] = tot.astype(BF16)
        if g > 0:
            pt[g] = tot.T.astype(BF16)

        def asis(k, xd):
            return remote(pc.at[g], fin.at[g, y, l], send, recv, at(*spots[k], h, xd, c))

        def turned(k, sem):
            return remote(pt.at[g], fin.at[g, y, 2 + c], sem, recv_t, at(*spots[k], (h + far_set) % 2, x, l))

        def start(two):
            if not two:
                pltpu.make_async_copy(pc.at[g], fin.at[g, y, l], recv).start()
                for k in range(1, len(spots)):
                    asis(k, x).start()
                return
            for k in range(len(spots)):
                asis(k, (x + 3 - y % 2) % NX).start()
                if k > 0:
                    turned(k, send).start()
            if far_set:
                turned(0, send).start()
            else:
                @pl.when(c == l)
                def _():
                    pltpu.make_async_copy(pt.at[g], fin.at[g, y, 2 + c], recv_t).start()

                @pl.when(c != l)
                def _():
                    turned(0, cond_send).start()

        def sent(two):
            n = 2 * len(spots) if two else len(spots)
            if not two or not far_set:
                n -= 1
            got(slots(n), send)
            if two and not far_set:
                @pl.when(c != l)
                def _():
                    turned(0, cond_send).wait_send()

        for cond, two in kinds(g):
            under(cond, lambda two=two: start(two))
        wait_sent.append(lambda: [under(cond, lambda two=two: sent(two)) for cond, two in kinds(g)])

    wait_sent = []

    def along_y(g, dy):
        i, n = ZFIRST.index(g), 4 if g > 0 else 2
        mine = fin.at[g, y, pl.ds(0, n)]
        return remote(mine, mine, zf_s.at[i, 2], zf_r.at[i, 1], at(l, (y + dy) % NY, h, x, c))

    def spread(g):
        n = 4 if g > 0 else 2
        got(fin.at[g, y, pl.ds(0, n)], zf_r.at[ZFIRST.index(g), 0])
        for dy in range(1, NY):
            along_y(g, dy).start()

    def finish(g):
        i, n = ZFIRST.index(g), 4 if g > 0 else 2
        three = fin.at[g, pl.ds(0, 3), pl.ds(0, n)]
        got(three, zf_r.at[i, 1])
        got(three, zf_s.at[i, 2])

    def across(g, k):
        i = YFIRST.index(g)
        low = 2 if g in MIXED else 0
        view = fin.at[g, pl.ds(0, NY), l] if k == 0 else fin.at[g, pl.ds(low, NY - low), pl.ds(2, 2)]
        return remote(view, view, yf_s.at[i, 2 + k], yf_r.at[i, 2 if k == 0 else 1], at(1 - l, y, h, x, c)), view

    def cross_asis(g):
        cp, view = across(g, 0)
        got(view, yf_r.at[YFIRST.index(g), 0])
        cp.start()

    def cross_turned(g):
        @pl.when(c == l)
        def _():
            cp, view = across(g, 1)
            got(view, yf_r.at[YFIRST.index(g), 1])
            cp.start()

    def finish_late(g):
        i = YFIRST.index(g)
        got(fin.at[g, pl.ds(0, NY), 1 - l], yf_r.at[i, 2])
        cp, view = across(g, 1)

        @pl.when(c != l)
        def _():
            got(view, yf_r.at[i, 1])

        @pl.when(c == l)
        def _():
            cp.wait_send()
        across(g, 0)[0].wait_send()

    pass_f(2)
    go(to_e[3], to_e[4], *to_f[3:])
    scale(near.at[c], 0, xt, 0, cols)
    pass_z(0)
    to_core.wait_recv()
    scale(near.at[1 - c], 0, raw.at[0], 0, cols)
    near_own()
    sum_y_start(0)
    redp[...] = nt(kept[...], near[c])
    dsend = []
    for i, (dl, dy) in enumerate(ring3):
        tl, ty = (l + dl) % 2, (y + dy) % NY
        dsend.append(remote(redp.at[pl.ds(pl.multiple_of((tl * NY + ty) * 8, 8), 8)], redr.at[i], d_s.at[3], d_r.at[3],
                            at(tl, ty, h, x, c)))
    go(*dsend)
    scale_e(0)
    scale_e(1)
    scale_z(0)
    pass_z(1)
    sum_l_start(0)
    go(to_z[3], to_e[5], to_e[6])
    scale_e(2)
    take_f(0, 1, 2)
    near_ef(1, 0)
    sum_y_start(1)
    scale_z(1)
    far_with(2, 0, 0, near[c])
    far_with(2, 2, 0, ef[0])
    sum_y_start(2)
    publish(0)
    go(to_z[4])
    pass_f(3)
    pass_z(2)
    scale_e(3)
    scale_z(2)
    pass_f(4)
    sum_l_start(1)
    pass_z(3)
    pass_f(5)
    scale_z(3)
    sum_l_start(2)
    go(to_z[5])
    pass_f(6)
    scale_e(4)
    spread(0)
    take_f(3, 4)
    publish(1)
    publish(2)
    scale_e(5)
    scale_e(6)
    pass_z(4)
    take_f(5, 6)
    near_ef(3, 1)
    sum_start(3)
    scale_z(4)
    far_with(4, 0, 0, ef[1])
    pass_z(5)
    cross_asis(1)
    scale_z(5)
    far_with(4, 2, 1, ef[0])
    sum_start(4)
    publish(3)
    far_with(5, 0, 1, near[c])
    far_with(5, 2, 1, ef[1])
    sum_start(5)
    cross_turned(1)
    spread(3)
    publish(4)
    cross_asis(2)
    cross_turned(2)
    publish(5)
    spread(4)
    cross_asis(5)
    cross_turned(5)
    got(redr, d_r.at[3])
    tot = redp[pl.ds(pl.multiple_of(s * 8, 8), 8), :]
    for i in range(len(ring3)):
        tot = tot + redr[i]
    red_ref[...] = tot
    for g in range(SETS):
        (finish_late if g in YFIRST else finish)(g)

    for fn in wait_sent:
        fn()
    own_f = remote(xt.at[:, pl.ds(fs_mine, fk)], relay, bulk_s.at[0], bulk_r.at[0], left)
    own_f.wait_send()
    for ref, k in ((xt, 1), (xt, 2), (xt, 3), (xt, 4), (relay, 5)):
        got(ref, bulk_s.at[k])
    got(got1, st_s.at[0])
    got(got2, st_s.at[1])
    for g in range(EARLY):
        got(rs.at[g], rs_s.at[g])
        sum_l[g].wait_send()
    for g in range(SETS - EARLY):
        got(rd.at[g], d_s.at[g])
    got(redr, d_s.at[3])


def assemble(fin, red_in, gram, red_ref, held, block, in_sem, out_sem):
    _, _, h, x, _ = place()
    loads = [pltpu.make_async_copy(fin.at[g], held.at[g], in_sem.at[g]) for g in range(SETS)]
    for cp in loads:
        cp.start()
    red_ref[...] = red_in[...]

    def tile(step, nf, half, row, col):
        return step, (h + nf) % 2, pl.ds(half * 256 + row * 128, 128), pl.ds(col * 128, 128)

    for cp in loads:
        cp.wait()
    for step in (0, 1, 3, 2):
        for g in range(SETS):
            for y in range(NY):
                nf, kind, ra, cb = role(g, y)
                for j in range(2):
                    if kind == step:
                        block[tile(step, nf, j, ra, cb)] = held[g, y, j].astype(F32)
                    if kind == 1 and step == 3:
                        block[tile(step, nf, j, cb, ra)] = held[g, y, 2 + j].astype(F32)
        if step == 2:
            for g in range(SETS):
                for y in range(NY):
                    nf, kind, ra, cb = role(g, y)
                    if kind == 2:
                        for j in range(2):
                            block[tile(step, nf, j, cb, ra)] += held[g, y, 2 + j].astype(F32)
        pltpu.make_async_copy(block.at[step], gram.at[:, (x + step) % NX], out_sem.at[step]).start()
    for step in range(NX):
        pltpu.make_async_copy(block.at[step], gram.at[:, (x + step) % NX], out_sem.at[step]).wait()


def local(snapshots, var_index, modes, retained):
    rows, cols = snapshots.shape
    n_space, n_time = lax.axis_size("space"), lax.axis_size("tm")
    total_rows = rows * n_space
    count = float(total_rows // VARS * (cols * n_time))
    root = float(total_rows) ** 0.5
    r = modes.shape[1]
    fk = (rows // 128 + 1) // 2 * 128
    dma = pltpu.SemaphoreType.DMA

    def body(*refs):
        kernel(count, root, fk, *refs)

    vmem = pl.BlockSpec(memory_space=pltpu.VMEM)
    fin, red = pl.pallas_call(
        body,
        name="gram",
        out_shape=(jax.ShapeDtypeStruct((SETS, NY, 4, 128, 128), BF16), jax.ShapeDtypeStruct((r // n_space, cols), F32)),
        in_specs=[vmem, vmem, vmem, pl.BlockSpec(memory_space=pltpu.SMEM)],
        out_specs=(pl.BlockSpec(memory_space=pl.ANY), vmem),
        scratch_shapes=[
            pltpu.VMEM((cols, rows), BF16),
            pltpu.VMEM((3, cols, rows), BF16),
            pltpu.VMEM((cols, rows), BF16),
            pltpu.VMEM((cols, fk), BF16),
            pltpu.VMEM((cols, fk), BF16),
            pltpu.VMEM((2, cols, rows), BF16),
            pltpu.VMEM((2, 2, 128, rows), BF16),
            pltpu.VMEM((2, 256, rows), BF16),
            pltpu.VMEM((VARS, rows), F32),
            pltpu.VMEM((1, rows), F32),
            pltpu.VMEM((1, rows), F32),
            pltpu.VMEM((r, rows), BF16),
            pltpu.VMEM((VARS, 128), F32),
            pltpu.VMEM((VARS, 128), F32),
            pltpu.VMEM((7, VARS, 128), F32),
            pltpu.VMEM((15, VARS, 128), F32),
            pltpu.VMEM((SETS, NY, 2, 128, 128), F32),
            pltpu.VMEM((SETS, NY, 2, 128, 128), BF16),
            pltpu.VMEM((EARLY, NY - 1, 2, 128, 128), BF16),
            pltpu.VMEM((EARLY, 2, 128, 128), F32),
            pltpu.VMEM((EARLY, 128, 128), F32),
            pltpu.VMEM((r, cols), F32),
            pltpu.VMEM((7, 8, cols), F32),
            pltpu.VMEM((SETS, 128, 128), BF16),
            pltpu.VMEM((SETS, 128, 128), BF16),
            pltpu.VMEM((SETS - EARLY, 7, 128, 128), BF16),
            dma((6,)), dma((3 * (len(CUTS) - 1) + 2 * (len(ZCUTS) - 1) + 1,)), dma((2,)), dma((2,)),
            dma((EARLY,)), dma((EARLY,)), dma((EARLY,)), dma((EARLY,)), dma((4,)), dma((4,)),
            dma((3, 3)), dma((3, 2)), dma((3, 4)), dma((3, 3)),
        ],
        compiler_params=pltpu.CompilerParams(
            collective_id=0, has_side_effects=True, vmem_limit_bytes=60 * 2 ** 20),
    )(snapshots, var_index, modes.T, retained)
    gram, red = pl.pallas_call(
        assemble,
        name="columns",
        in_specs=[pl.BlockSpec(memory_space=pl.ANY), vmem],
        out_specs=(pl.BlockSpec(memory_space=pl.ANY), vmem),
        out_shape=(jax.ShapeDtypeStruct((2, NX, 2 * cols, cols), F32), jax.ShapeDtypeStruct(red.shape, F32)),
        scratch_shapes=[pltpu.VMEM(fin.shape, BF16), pltpu.VMEM((NX, 2, 2 * cols, cols), F32), dma((SETS,)), dma((NX,))],
        compiler_params=pltpu.CompilerParams(vmem_limit_bytes=60 * 2 ** 20),
    )(fin, red)
    return gram.reshape(cols * n_time, cols), red


def solution(mesh):
    return jax.shard_map(
        local,
        mesh=mesh,
        in_specs=(P("space", "tm"), P("space"), P("space", None), P()),
        out_specs=(P(None, "tm"), P("space", "tm")),
        check_vma=False,
    )
```

```python
import jax
import jax.numpy as jnp
from jax import lax
from jax.experimental import pallas as pl
from jax.experimental.pallas import tpu as pltpu
from jax.sharding import PartitionSpec as P

MESH = pl.DeviceIdType.MESH
VARS = 8
NY, NX = 4, 4
F32, BF16 = jnp.float32, jnp.bfloat16


def place():
    s, t = lax.axis_index("space"), lax.axis_index("tm")
    return s // NY, s % NY, t // 8, (t // 2) % NX, t % 2


def at(l, y, h, x, c):
    return (l * NY + y, h * 8 + x * 2 + c)


def nt(a, b):
    return lax.dot_general(a, b, (((1,), (1,)), ((), ())), preferred_element_type=F32)


def pack(n, total, squares):
    lane = lax.broadcasted_iota(jnp.int32, (VARS, 128), 1)
    return jnp.where(lane == 0, n, jnp.where(lane == 1, total, squares))


def merge(tiles):
    n = sum(t[:, 0:1] for t in tiles)
    total = sum(t[:, 1:2] for t in tiles)
    mean = total / jnp.maximum(n, 1.0)
    squares = jnp.zeros_like(n)
    for t in tiles:
        off = t[:, 1:2] / jnp.maximum(t[:, 0:1], 1.0) - mean
        squares = squares + t[:, 2:3] + t[:, 0:1] * off * off
    return n, total, squares


def role(g, y):
    two, odd = y // 2, y % 2
    if g == 0:
        return 0, 0, two, odd
    if g in (1, 3):
        return 0, 1 + odd, two, g // 2
    if g == 4:
        return 1, 1 + odd, two, 1 - two
    last = g // 3
    return (1, 0, last, odd) if two == 0 else (1, 1 + odd, last, last)


SETS = 6
MIXED = (2, 5)
EARLY = 3
YFIRST = (1, 2, 5)
ZFIRST = (0, 3, 4)
CUTS = (0, 16, 64, 128, 160, 192, 224, 256)
ZCUTS = (0, 64, 128, 160, 192, 224, 256)


def kernel(count, root, fk, x_hbm, vi_hbm, modes_hbm, ret_ref, fin, red_ref,
           x_ref, vi_ref, modes_ref, load, xt, raw, rawe, relay, rawf, near, far, ef, hot, mean_l, inv_l, kept,
           tile1, tile2, got1, got2, ps, cs, rs, tmp, r2, redp, redr, pc, pt,
           rd, bulk_s, bulk_r, st_s, st_r, rs_s, rs_r, r2_s, r2_r, d_s, d_r, zf_s, zf_r, yf_s, yf_r):
    l, y, h, x, c = place()
    s = l * NY + y
    rows = xt.shape[1]
    cols = xt.shape[0]
    ntile = rows // 128

    ring1 = [(dx, dc) for dx in range(NX) for dc in range(2) if (dx, dc) != (0, 0)]
    ring2 = [(dy, dl, dh) for dy in range(NY) for dl in range(2) for dh in range(2) if (dy, dl, dh) != (0, 0, 0)]

    def dev1(dx, dc):
        return at(l, y, h, (x + dx) % NX, (c + dc) % 2)

    def dev2(dy, dl, dh):
        return at((l + dl) % 2, (y + dy) % NY, (h + dh) % 2, x, c)

    lanes = [pl.ds(128 * half, 128) for half in range(2)]
    x_loads = [pltpu.make_async_copy(x_hbm.at[:, r], x_ref.at[:, r], load.at[half]) for half, r in enumerate(lanes)]
    vi_load = pltpu.make_async_copy(vi_hbm, vi_ref, load.at[2])
    modes_load = pltpu.make_async_copy(modes_hbm, modes_ref, load.at[3])
    for cp in x_loads + [vi_load, modes_load]:
        cp.start()
    barrier = pltpu.get_barrier_semaphore()
    for d in ring1:
        pl.semaphore_signal(barrier, inc=1, device_id=dev1(*d), device_id_type=MESH)
    for d in ring2:
        pl.semaphore_signal(barrier, inc=1, device_id=dev2(*d), device_id_type=MESH)

    def turn(half):
        x_loads[half].wait()
        for k in range(ntile):
            xt[128 * half:128 * half + 128, 128 * k:128 * k + 128] = x_ref[128 * k:128 * k + 128, 128 * half:128 * half + 128].T

    turn(0)
    pl.semaphore_wait(barrier, len(ring1) + len(ring2))

    def remote(src, dst, ss, rsem, dev):
        return pltpu.make_async_remote_copy(src, dst, ss, rsem, device_id=dev, device_id_type=MESH)

    def go(*copies):
        for cp in copies:
            cp.start()

    def got(ref, sem):
        pltpu.make_async_copy(ref, ref, sem).wait()

    fs_mine = pl.multiple_of((x // 2) * (rows - fk), 128)
    parts = [pl.ds(lo, hi - lo) for lo, hi in zip(CUTS, CUTS[1:])]
    to_f, to_e, to_z, to_core, to_diag, fwd = [], [], [], [], [], []
    left, core = at(l, y, h, (x + NX - 1) % NX, c), at(l, y, h, x, 1 - c)
    nf, nz = len(CUTS) - 1, len(ZCUTS) - 1
    for k, r in enumerate(parts):
        to_f.append(remote(xt.at[r, pl.ds(fs_mine, fk)], relay.at[r], bulk_s.at[0], bulk_r.at[k], left))
        to_e.append(remote(xt.at[r], rawe.at[r], bulk_s.at[1], bulk_r.at[nf + k], at(l, y, h, (x + 1) % NX, c)))
        fwd.append(remote(relay.at[r], rawf.at[r], bulk_s.at[5], bulk_r.at[2 * nf + k], left))
    for k, r in enumerate([pl.ds(lo, hi - lo) for lo, hi in zip(ZCUTS, ZCUTS[1:])]):
        to_z.append(remote(xt.at[r], raw.at[1, r], bulk_s.at[2], bulk_r.at[3 * nf + k], at(l, y, 1 - h, x, c)))
        to_diag.append(remote(raw.at[1, r], raw.at[2, r], bulk_s.at[4], bulk_r.at[3 * nf + nz + k], core))
    to_core = remote(xt, raw.at[0], bulk_s.at[3], bulk_r.at[3 * nf + 2 * nz], core)

    def pass_f(*ks):
        for k in ks:
            to_f[k].wait_recv()
            go(fwd[k])

    go(to_f[0], to_e[0], to_z[0])
    turn(1)
    go(to_core)

    vi_load.wait()
    hot[...] = (vi_ref[...][None, :] == lax.broadcasted_iota(jnp.int32, (VARS, rows), 0)).astype(F32)

    def colsum(fn):
        def body(k, acc):
            blk = xt[pl.ds(pl.multiple_of(k * 16, 16), 16), :].astype(F32)
            return acc + fn(blk)
        acc = lax.fori_loop(0, cols // 16, body, jnp.zeros((16, rows), F32))
        return jnp.sum(acc, axis=0, keepdims=True)

    n1 = jnp.sum(hot[...], axis=1, keepdims=True) * cols
    sum1 = jnp.sum(hot[...] * colsum(lambda b: b), axis=1, keepdims=True)
    m1 = sum1 / jnp.maximum(n1, 1.0)
    mean_l[...] = jnp.sum(hot[...] * m1, axis=0, keepdims=True)

    def sq(b):
        d = b - mean_l[...]
        return d * d
    sq1 = jnp.sum(hot[...] * colsum(sq), axis=1, keepdims=True)
    tile1[...] = pack(n1, sum1, sq1)
    sends1 = [remote(tile1, got1.at[i], st_s.at[0], st_r.at[0], dev1(*d)) for i, d in enumerate(ring1)]
    go(*sends1)
    go(to_f[1], to_e[1], to_f[2], to_e[2])
    modes_load.wait()
    keep = lax.broadcasted_iota(jnp.int32, kept.shape, 0) < ret_ref[0]
    kept[...] = jnp.where(keep, modes_ref[...].astype(F32), 0.0).astype(BF16)
    for half in range(2):
        ef[half, 128:256, :] = jnp.zeros((128, rows), BF16)
    got(got1, st_r.at[0])
    pass_f(0)
    n2, sum2, sq2 = merge([tile1[...]] + [got1[i] for i in range(len(ring1))])
    tile2[...] = pack(n2, sum2, sq2)
    sends2 = [remote(tile2, got2.at[i], st_s.at[1], st_r.at[1], dev2(*d)) for i, d in enumerate(ring2)]
    go(*sends2)
    go(to_z[1])
    pass_f(1)
    got(got2, st_r.at[1])
    _, sum3, sq3 = merge([tile2[...]] + [got2[i] for i in range(len(ring2))])
    mean = sum3 / count
    inv = 1.0 / jnp.sqrt(sq3 / count + 1e-06)
    mean_l[...] = jnp.sum(hot[...] * mean, axis=0, keepdims=True)
    inv_l[...] = jnp.sum(hot[...] * inv, axis=0, keepdims=True)
    go(to_z[2])

    def scale_to(dst, dlo, src, lo, n, m, v):
        def body(k, _):
            a = pl.multiple_of(k * 16, 16)
            dst[pl.ds(dlo + a, 16), :] = ((src[pl.ds(lo + a, 16), :].astype(F32) - m) * v).astype(BF16)
            return 0
        lax.fori_loop(0, n // 16, body, 0)

    def scale(dst, dlo, src, lo, n):
        scale_to(dst, dlo, src, lo, n, mean_l[...], inv_l[...])

    fs = pl.multiple_of((((x + 2) % NX) // 2) * (rows - fk), 128)
    fl = pl.ds(fs, fk)
    over = 2 * fk - rows
    first = lax.broadcasted_iota(jnp.int32, (1, fk), 1) < over
    drop = jnp.logical_and(first, x < 2)

    def scale_f(k):
        half, lo = CUTS[k] // 128, CUTS[k] % 128
        scale_to(ef.at[half, :, fl], 128 + lo, rawf, CUTS[k], CUTS[k + 1] - CUTS[k], mean_l[:, fl],
                 jnp.where(drop, 0.0, inv_l[:, fl]))

    def pass_z(k):
        to_z[k].wait_recv()
        go(to_diag[k])

    def scale_z(k):
        half, lo, n = ZCUTS[k] // 128, ZCUTS[k] % 128, ZCUTS[k + 1] - ZCUTS[k]
        scale(far.at[half, c], lo, raw.at[1], ZCUTS[k], n)
        to_diag[k].wait_recv()
        scale(far.at[half, 1 - c], lo, raw.at[2], ZCUTS[k], n)

    def take_f(*ks):
        for k in ks:
            fwd[k].wait_recv()
            scale_f(k)

    def scale_e(k):
        half, lo, n = CUTS[k] // 128, CUTS[k] % 128, CUTS[k + 1] - CUTS[k]
        to_e[k].wait_recv()
        scale(ef.at[half], lo, rawe, CUTS[k], n)

    def near_own():
        for cc in range(2):
            p = nt(near[cc], near[c])
            for k in range(4):
                ps[0, k, cc] = p[128 * (k // 2):128 * (k // 2) + 128, 128 * (k % 2):128 * (k % 2) + 128]

    def near_ef(g, half):
        for cc in range(2):
            p = nt(near[cc], ef[half])
            for k in range(4):
                ps[g, k, cc] = p[128 * (k // 2):128 * (k // 2) + 128, 128 * (k % 2):128 * (k % 2) + 128]

    def far_with(g, slot, ra, right):
        p = nt(far[ra].reshape(256, rows), right)
        for cc in range(2):
            for k in range(2):
                ps[g, slot + k, cc] = p[128 * cc:128 * cc + 128, 128 * k:128 * k + 128]

    def sum_y_start(g):
        cs[g] = ps[g].astype(BF16)
        go(*sum_y[g])

    sum_y = [[remote(cs.at[g, (y + dy) % NY], rs.at[g, dy - 1], rs_s.at[g], rs_r.at[g],
                     at(l, (y + dy) % NY, h, x, c)) for dy in range(1, NY)] for g in range(EARLY)]
    sum_l = [remote(tmp.at[g, 1 - l], r2.at[g], r2_s.at[g], r2_r.at[g], at(1 - l, y, h, x, c)) for g in range(EARLY)]

    ring3 = [(dl, dy) for dl in range(2) for dy in range(NY) if (dl, dy) != (0, 0)]
    sum_s = {}
    for g in range(EARLY, SETS):
        sum_s[g] = [remote(cs.at[g, (y + dy) % NY, (l + dl) % 2], rd.at[g - EARLY, i], d_s.at[g - EARLY], d_r.at[g - EARLY],
                           at((l + dl) % 2, (y + dy) % NY, h, x, c)) for i, (dl, dy) in enumerate(ring3)]

    def sum_start(g):
        cs[g] = ps[g].astype(BF16)
        go(*sum_s[g])

    def total(g):
        if g < EARLY:
            sum_l[g].wait_recv()
            tot = tmp[g, l] + r2[g]
        else:
            got(rd.at[g - EARLY], d_r.at[g - EARLY])
            tot = ps[g, y, l]
            for i in range(len(ring3)):
                tot = tot + rd[g - EARLY, i].astype(F32)
        return tot * (1.0 / root)

    def sum_l_start(g):
        got(rs.at[g], rs_r.at[g])
        tot = ps[g, y]
        for k in range(NY - 1):
            tot = tot + rs[g, k].astype(F32)
        tmp[g] = tot
        go(sum_l[g])

    def kinds(g):
        if g == 0:
            return [(None, False)]
        if g in MIXED:
            return [(y < 2, False), (y >= 2, True)]
        return [(None, True)]

    def under(cond, fn):
        if cond is None:
            fn()
        else:
            pl.when(cond)(fn)

    def slots(n):
        return cs.at[0] if n == 8 else rd.at[0, pl.ds(0, n)]

    def publish(g):
        zf = g in ZFIRST
        i = (ZFIRST if zf else YFIRST).index(g)
        send, cond_send = (zf_s.at[i, 0], zf_s.at[i, 1]) if zf else (yf_s.at[i, 0], yf_s.at[i, 1])
        recv, recv_t = (zf_r.at[i, 0], zf_r.at[i, 0]) if zf else (yf_r.at[i, 0], yf_r.at[i, 1])
        far_set = role(g, 3)[0]
        spots = [((l + k) % 2, y) for k in range(2)] if zf else [(l, (y + k) % NY) for k in range(NY)]
        tot = total(g)
        pc[g] = tot.astype(BF16)
        if g > 0:
            pt[g] = tot.T.astype(BF16)

        def asis(k, xd):
            return remote(pc.at[g], fin.at[g, y, l], send, recv, at(*spots[k], h, xd, c))

        def turned(k, sem):
            tl, ty = spots[k]
            if far_set and not zf:
                tl = 1 - l
            return remote(pt.at[g], fin.at[g, y, 2 + c], sem, recv_t, at(tl, ty, (h + far_set) % 2, x, l))

        def start(two):
            if not two:
                pltpu.make_async_copy(pc.at[g], fin.at[g, y, l], recv).start()
                for k in range(1, len(spots)):
                    asis(k, x).start()
                return
            for k in range(len(spots)):
                asis(k, (x + 3 - y % 2) % NX).start()
                if k > 0:
                    turned(k, send).start()
            if far_set:
                turned(0, send).start()
            else:
                @pl.when(c == l)
                def _():
                    pltpu.make_async_copy(pt.at[g], fin.at[g, y, 2 + c], recv_t).start()

                @pl.when(c != l)
                def _():
                    turned(0, cond_send).start()

        def sent(two):
            n = 2 * len(spots) if two else len(spots)
            if not two or not far_set:
                n -= 1
            got(slots(n), send)
            if two and not far_set:
                @pl.when(c != l)
                def _():
                    turned(0, cond_send).wait_send()

        for cond, two in kinds(g):
            under(cond, lambda two=two: start(two))
        wait_sent.append(lambda: [under(cond, lambda two=two: sent(two)) for cond, two in kinds(g)])

    wait_sent = []

    def along_y(g, dy):
        i, n = ZFIRST.index(g), 4 if g > 0 else 2
        mine = fin.at[g, y, pl.ds(0, n)]
        return remote(mine, mine, zf_s.at[i, 2], zf_r.at[i, 1], at(l, (y + dy) % NY, h, x, c))

    def spread(g):
        n = 4 if g > 0 else 2
        got(fin.at[g, y, pl.ds(0, n)], zf_r.at[ZFIRST.index(g), 0])
        for dy in range(1, NY):
            along_y(g, dy).start()

    def finish(g):
        i, n = ZFIRST.index(g), 4 if g > 0 else 2
        three = fin.at[g, pl.ds(0, 3), pl.ds(0, n)]
        got(three, zf_r.at[i, 1])
        got(three, zf_s.at[i, 2])

    def across(g, k):
        i = YFIRST.index(g)
        low = 2 if g in MIXED else 0
        view = fin.at[g, pl.ds(0, NY), l] if k == 0 else fin.at[g, pl.ds(low, NY - low), pl.ds(2, 2)]
        return remote(view, view, yf_s.at[i, 2 + k], yf_r.at[i, 2 if k == 0 else 1], at(1 - l, y, h, x, c)), view

    def cross_asis(g):
        cp, view = across(g, 0)
        got(view, yf_r.at[YFIRST.index(g), 0])
        cp.start()

    def first_hand(g):
        return c != l if role(g, 3)[0] else c == l

    def cross_turned(g):
        @pl.when(first_hand(g))
        def _():
            cp, view = across(g, 1)
            got(view, yf_r.at[YFIRST.index(g), 1])
            cp.start()

    def finish_late(g):
        i = YFIRST.index(g)
        got(fin.at[g, pl.ds(0, NY), 1 - l], yf_r.at[i, 2])
        cp, view = across(g, 1)

        @pl.when(jnp.logical_not(first_hand(g)))
        def _():
            got(view, yf_r.at[i, 1])

        @pl.when(first_hand(g))
        def _():
            cp.wait_send()
        across(g, 0)[0].wait_send()

    pass_f(2)
    go(to_e[3], to_e[4], *to_f[3:])
    scale(near.at[c], 0, xt, 0, cols)
    pass_z(0)
    to_core.wait_recv()
    scale(near.at[1 - c], 0, raw.at[0], 0, cols)
    near_own()
    sum_y_start(0)
    redp[...] = nt(kept[...], near[c])
    dsend = []
    for i, (dl, dy) in enumerate(ring3):
        tl, ty = (l + dl) % 2, (y + dy) % NY
        dsend.append(remote(redp.at[pl.ds(pl.multiple_of((tl * NY + ty) * 8, 8), 8)], redr.at[i], d_s.at[3], d_r.at[3],
                            at(tl, ty, h, x, c)))
    go(*dsend)
    scale_e(0)
    scale_e(1)
    scale_z(0)
    pass_z(1)
    sum_l_start(0)
    go(to_z[3], to_e[5], to_e[6])
    scale_e(2)
    take_f(0, 1, 2)
    near_ef(1, 0)
    sum_y_start(1)
    scale_z(1)
    far_with(2, 0, 0, near[c])
    far_with(2, 2, 0, ef[0])
    sum_y_start(2)
    publish(0)
    go(to_z[4])
    pass_f(3)
    pass_z(2)
    scale_e(3)
    scale_z(2)
    pass_f(4)
    sum_l_start(1)
    pass_z(3)
    pass_f(5)
    scale_z(3)
    sum_l_start(2)
    go(to_z[5])
    pass_f(6)
    scale_e(4)
    spread(0)
    take_f(3, 4)
    publish(1)
    publish(2)
    scale_e(5)
    scale_e(6)
    pass_z(4)
    take_f(5, 6)
    near_ef(3, 1)
    sum_start(3)
    scale_z(4)
    far_with(4, 0, 0, ef[1])
    pass_z(5)
    cross_asis(1)
    scale_z(5)
    far_with(4, 2, 1, ef[0])
    sum_start(4)
    far_with(5, 0, 1, near[c])
    far_with(5, 2, 1, ef[1])
    publish(3)
    sum_start(5)
    spread(3)
    publish(4)
    cross_turned(1)
    cross_asis(2)
    publish(5)
    cross_turned(2)
    spread(4)
    cross_asis(5)
    cross_turned(5)
    got(redr, d_r.at[3])
    tot = redp[pl.ds(pl.multiple_of(s * 8, 8), 8), :]
    for i in range(len(ring3)):
        tot = tot + redr[i]
    red_ref[...] = tot
    for g in range(SETS):
        (finish_late if g in YFIRST else finish)(g)

    for fn in wait_sent:
        fn()
    own_f = remote(xt.at[:, pl.ds(fs_mine, fk)], relay, bulk_s.at[0], bulk_r.at[0], left)
    own_f.wait_send()
    for ref, k in ((xt, 1), (xt, 2), (xt, 3), (xt, 4), (relay, 5)):
        got(ref, bulk_s.at[k])
    got(got1, st_s.at[0])
    got(got2, st_s.at[1])
    for g in range(EARLY):
        got(rs.at[g], rs_s.at[g])
        sum_l[g].wait_send()
    for g in range(SETS - EARLY):
        got(rd.at[g], d_s.at[g])
    got(redr, d_s.at[3])


def assemble(fin, red_in, gram, red_ref, block, out_sem):
    _, _, h, x, _ = place()
    red_ref[...] = red_in[...]

    def tile(step, nf, half, row, col):
        return step, (h + nf) % 2, pl.ds(half * 256 + row * 128, 128), pl.ds(col * 128, 128)

    def store(step, half):
        return pltpu.make_async_copy(block.at[step, half], gram.at[half, (x + step) % NX], out_sem.at[2 * step + half])

    for step in (0, 1, 3, 2):
        for g in range(SETS):
            for y in range(NY):
                nf, kind, ra, cb = role(g, y)
                for j in range(2):
                    if kind == step:
                        block[tile(step, nf, j, ra, cb)] = fin[g, y, j].astype(F32)
                    if kind == 1 and step == 3:
                        block[tile(step, nf, j, cb, ra)] = fin[g, y, 2 + j].astype(F32)
        if step == 2:
            for g in range(SETS):
                for y in range(NY):
                    nf, kind, ra, cb = role(g, y)
                    if kind == 2:
                        for j in range(2):
                            block[tile(step, nf, j, cb, ra)] += fin[g, y, 2 + j].astype(F32)
        for half in range(2):
            store(step, half).start()
    for step in range(NX):
        for half in range(2):
            store(step, half).wait()


def local(snapshots, var_index, modes, retained):
    rows, cols = snapshots.shape
    n_space, n_time = lax.axis_size("space"), lax.axis_size("tm")
    total_rows = rows * n_space
    count = float(total_rows // VARS * (cols * n_time))
    root = float(total_rows) ** 0.5
    r = modes.shape[1]
    fk = (rows // 128 + 1) // 2 * 128
    dma = pltpu.SemaphoreType.DMA

    def body(*refs):
        kernel(count, root, fk, *refs)

    vmem = pl.BlockSpec(memory_space=pltpu.VMEM)
    fin, red = pl.pallas_call(
        body,
        name="gram",
        out_shape=(pltpu.VMEM((SETS, NY, 4, 128, 128), BF16), pltpu.VMEM((r // n_space, cols), F32)),
        in_specs=[pl.BlockSpec(memory_space=pltpu.HBM)] * 3 + [pl.BlockSpec(memory_space=pltpu.SMEM)],
        out_specs=(vmem, vmem),
        scratch_shapes=[
            pltpu.VMEM((rows, cols), BF16),
            pltpu.VMEM((rows,), jnp.int32),
            pltpu.VMEM((r, rows), BF16),
            dma((4,)),
            pltpu.VMEM((cols, rows), BF16),
            pltpu.VMEM((3, cols, rows), BF16),
            pltpu.VMEM((cols, rows), BF16),
            pltpu.VMEM((cols, fk), BF16),
            pltpu.VMEM((cols, fk), BF16),
            pltpu.VMEM((2, cols, rows), BF16),
            pltpu.VMEM((2, 2, 128, rows), BF16),
            pltpu.VMEM((2, 256, rows), BF16),
            pltpu.VMEM((VARS, rows), F32),
            pltpu.VMEM((1, rows), F32),
            pltpu.VMEM((1, rows), F32),
            pltpu.VMEM((r, rows), BF16),
            pltpu.VMEM((VARS, 128), F32),
            pltpu.VMEM((VARS, 128), F32),
            pltpu.VMEM((7, VARS, 128), F32),
            pltpu.VMEM((15, VARS, 128), F32),
            pltpu.VMEM((SETS, NY, 2, 128, 128), F32),
            pltpu.VMEM((SETS, NY, 2, 128, 128), BF16),
            pltpu.VMEM((EARLY, NY - 1, 2, 128, 128), BF16),
            pltpu.VMEM((EARLY, 2, 128, 128), F32),
            pltpu.VMEM((EARLY, 128, 128), F32),
            pltpu.VMEM((r, cols), F32),
            pltpu.VMEM((7, 8, cols), F32),
            pltpu.VMEM((SETS, 128, 128), BF16),
            pltpu.VMEM((SETS, 128, 128), BF16),
            pltpu.VMEM((SETS - EARLY, 7, 128, 128), BF16),
            dma((6,)), dma((3 * (len(CUTS) - 1) + 2 * (len(ZCUTS) - 1) + 1,)), dma((2,)), dma((2,)),
            dma((EARLY,)), dma((EARLY,)), dma((EARLY,)), dma((EARLY,)), dma((4,)), dma((4,)),
            dma((3, 3)), dma((3, 2)), dma((3, 4)), dma((3, 3)),
        ],
        compiler_params=pltpu.CompilerParams(
            collective_id=0, has_side_effects=True, vmem_limit_bytes=59 * 2 ** 20),
    )(snapshots, var_index, modes.T, retained)
    gram, red = pl.pallas_call(
        assemble,
        name="columns",
        in_specs=[vmem, vmem],
        out_specs=(pl.BlockSpec(memory_space=pl.ANY), vmem),
        out_shape=(jax.ShapeDtypeStruct((2, NX, 2 * cols, cols), F32), jax.ShapeDtypeStruct(red.shape, F32)),
        scratch_shapes=[pltpu.VMEM((NX, 2, 2 * cols, cols), F32), dma((2 * NX,))],
        compiler_params=pltpu.CompilerParams(vmem_limit_bytes=40 * 2 ** 20),
    )(fin, red)
    return gram.reshape(cols * n_time, cols), red


def solution(mesh):
    return jax.shard_map(
        local,
        mesh=mesh,
        in_specs=(P("space", "tm"), P("space"), P("space", None), P()),
        out_specs=(P(None, "tm"), P("space", "tm")),
        check_vma=False,
    )
```

```python
import jax
import jax.numpy as jnp
from jax import lax
from jax.experimental import pallas as pl
from jax.experimental.pallas import tpu as pltpu
from jax.sharding import PartitionSpec as P

MESH = pl.DeviceIdType.MESH
VARS = 8
NY, NX = 4, 4
F32, BF16 = jnp.float32, jnp.bfloat16


def place():
    s, t = lax.axis_index("space"), lax.axis_index("tm")
    return s // NY, s % NY, t // 8, (t // 2) % NX, t % 2


def at(l, y, h, x, c):
    return (l * NY + y, h * 8 + x * 2 + c)


def nt(a, b):
    return lax.dot_general(a, b, (((1,), (1,)), ((), ())), preferred_element_type=F32)


def pack(n, total, squares):
    lane = lax.broadcasted_iota(jnp.int32, (VARS, 128), 1)
    return jnp.where(lane == 0, n, jnp.where(lane == 1, total, squares))


def merge(tiles):
    n = sum(t[:, 0:1] for t in tiles)
    total = sum(t[:, 1:2] for t in tiles)
    mean = total / jnp.maximum(n, 1.0)
    squares = jnp.zeros_like(n)
    for t in tiles:
        off = t[:, 1:2] / jnp.maximum(t[:, 0:1], 1.0) - mean
        squares = squares + t[:, 2:3] + t[:, 0:1] * off * off
    return n, total, squares


def role(g, y):
    two, odd = y // 2, y % 2
    if g == 0:
        return 0, 0, two, odd
    if g in (1, 3):
        return 0, 1 + odd, two, g // 2
    if g == 4:
        return 1, 1 + odd, two, 1 - two
    last = g // 3
    return (1, 0, last, odd) if two == 0 else (1, 1 + odd, last, last)


SETS = 6
MIXED = (2, 5)
EARLY = 3
YFIRST = (1, 2, 5)
ZFIRST = (0, 3, 4)
CUTS = (0, 16, 64, 128, 160, 192, 224, 256)
ZCUTS = (0, 64, 128, 160, 192, 224, 256)


def kernel(count, root, fk, x_hbm, vi_hbm, modes_hbm, ret_ref, fin, red_ref,
           x_ref, vi_ref, modes_ref, load, xt, raw, rawe, relay, rawf, near, far, ef, hot, mean_l, inv_l, kept,
           tile1, tile2, got1, got2, ps, cs, rs, tmp, r2, redp, redr, pc, pt,
           rd, bulk_s, bulk_r, st_s, st_r, rs_s, rs_r, r2_s, r2_r, d_s, d_r, zf_s, zf_r, yf_s, yf_r):
    l, y, h, x, c = place()
    s = l * NY + y
    rows = xt.shape[1]
    cols = xt.shape[0]
    ntile = rows // 128

    ring1 = [(dx, dc) for dx in range(NX) for dc in range(2) if (dx, dc) != (0, 0)]
    ring2 = [(dy, dl, dh) for dy in range(NY) for dl in range(2) for dh in range(2) if (dy, dl, dh) != (0, 0, 0)]

    def dev1(dx, dc):
        return at(l, y, h, (x + dx) % NX, (c + dc) % 2)

    def dev2(dy, dl, dh):
        return at((l + dl) % 2, (y + dy) % NY, (h + dh) % 2, x, c)

    lanes = [pl.ds(128 * half, 128) for half in range(2)]
    x_loads = [pltpu.make_async_copy(x_hbm.at[:, r], x_ref.at[:, r], load.at[half]) for half, r in enumerate(lanes)]
    vi_load = pltpu.make_async_copy(vi_hbm, vi_ref, load.at[2])
    modes_load = pltpu.make_async_copy(modes_hbm, modes_ref, load.at[3])
    for cp in x_loads + [vi_load, modes_load]:
        cp.start()
    barrier = pltpu.get_barrier_semaphore()
    for d in ring1:
        pl.semaphore_signal(barrier, inc=1, device_id=dev1(*d), device_id_type=MESH)
    for d in ring2:
        pl.semaphore_signal(barrier, inc=1, device_id=dev2(*d), device_id_type=MESH)

    def turn(half):
        x_loads[half].wait()
        for k in range(ntile):
            xt[128 * half:128 * half + 128, 128 * k:128 * k + 128] = x_ref[128 * k:128 * k + 128, 128 * half:128 * half + 128].T

    turn(0)
    pl.semaphore_wait(barrier, len(ring1) + len(ring2))

    def remote(src, dst, ss, rsem, dev):
        return pltpu.make_async_remote_copy(src, dst, ss, rsem, device_id=dev, device_id_type=MESH)

    def go(*copies):
        for cp in copies:
            cp.start()

    def got(ref, sem):
        pltpu.make_async_copy(ref, ref, sem).wait()

    fs_mine = pl.multiple_of((x // 2) * (rows - fk), 128)
    parts = [pl.ds(lo, hi - lo) for lo, hi in zip(CUTS, CUTS[1:])]
    to_f, to_e, to_z, to_core, to_diag, fwd = [], [], [], [], [], []
    left, core = at(l, y, h, (x + NX - 1) % NX, c), at(l, y, h, x, 1 - c)
    nf, nz = len(CUTS) - 1, len(ZCUTS) - 1
    for k, r in enumerate(parts):
        to_f.append(remote(xt.at[r, pl.ds(fs_mine, fk)], relay.at[r], bulk_s.at[0], bulk_r.at[k], left))
        to_e.append(remote(xt.at[r], rawe.at[r], bulk_s.at[1], bulk_r.at[nf + k], at(l, y, h, (x + 1) % NX, c)))
        fwd.append(remote(relay.at[r], rawf.at[r], bulk_s.at[5], bulk_r.at[2 * nf + k], left))
    for k, r in enumerate([pl.ds(lo, hi - lo) for lo, hi in zip(ZCUTS, ZCUTS[1:])]):
        to_z.append(remote(xt.at[r], raw.at[1, r], bulk_s.at[2], bulk_r.at[3 * nf + k], at(l, y, 1 - h, x, c)))
        to_diag.append(remote(raw.at[1, r], raw.at[2, r], bulk_s.at[4], bulk_r.at[3 * nf + nz + k], core))
    to_core = remote(xt, raw.at[0], bulk_s.at[3], bulk_r.at[3 * nf + 2 * nz], core)

    def pass_f(*ks):
        for k in ks:
            to_f[k].wait_recv()
            go(fwd[k])

    go(to_f[0], to_e[0], to_z[0])
    turn(1)
    go(to_core)

    vi_load.wait()
    hot[...] = (vi_ref[...][None, :] == lax.broadcasted_iota(jnp.int32, (VARS, rows), 0)).astype(F32)

    def colsum(fn):
        def body(k, acc):
            blk = xt[pl.ds(pl.multiple_of(k * 16, 16), 16), :].astype(F32)
            return acc + fn(blk)
        acc = lax.fori_loop(0, cols // 16, body, jnp.zeros((16, rows), F32))
        return jnp.sum(acc, axis=0, keepdims=True)

    n1 = jnp.sum(hot[...], axis=1, keepdims=True) * cols
    sum1 = jnp.sum(hot[...] * colsum(lambda b: b), axis=1, keepdims=True)
    m1 = sum1 / jnp.maximum(n1, 1.0)
    mean_l[...] = jnp.sum(hot[...] * m1, axis=0, keepdims=True)

    def sq(b):
        d = b - mean_l[...]
        return d * d
    sq1 = jnp.sum(hot[...] * colsum(sq), axis=1, keepdims=True)
    tile1[...] = pack(n1, sum1, sq1)
    sends1 = [remote(tile1, got1.at[i], st_s.at[0], st_r.at[0], dev1(*d)) for i, d in enumerate(ring1)]
    go(*sends1)
    go(to_f[1], to_e[1], to_f[2], to_e[2])
    modes_load.wait()
    keep = lax.broadcasted_iota(jnp.int32, kept.shape, 0) < ret_ref[0]
    kept[...] = jnp.where(keep, modes_ref[...].astype(F32), 0.0).astype(BF16)
    for half in range(2):
        ef[half, 128:256, :] = jnp.zeros((128, rows), BF16)
    got(got1, st_r.at[0])
    pass_f(0)
    n2, sum2, sq2 = merge([tile1[...]] + [got1[i] for i in range(len(ring1))])
    tile2[...] = pack(n2, sum2, sq2)
    sends2 = [remote(tile2, got2.at[i], st_s.at[1], st_r.at[1], dev2(*d)) for i, d in enumerate(ring2)]
    go(*sends2)
    go(to_z[1])
    pass_f(1)
    got(got2, st_r.at[1])
    _, sum3, sq3 = merge([tile2[...]] + [got2[i] for i in range(len(ring2))])
    mean = sum3 / count
    inv = 1.0 / jnp.sqrt(sq3 / count + 1e-06)
    mean_l[...] = jnp.sum(hot[...] * mean, axis=0, keepdims=True)
    inv_l[...] = jnp.sum(hot[...] * inv, axis=0, keepdims=True)
    go(to_z[2])

    def scale_to(dst, dlo, src, lo, n, m, v):
        def body(k, _):
            a = pl.multiple_of(k * 16, 16)
            dst[pl.ds(dlo + a, 16), :] = ((src[pl.ds(lo + a, 16), :].astype(F32) - m) * v).astype(BF16)
            return 0
        lax.fori_loop(0, n // 16, body, 0)

    def scale(dst, dlo, src, lo, n):
        scale_to(dst, dlo, src, lo, n, mean_l[...], inv_l[...])

    fs = pl.multiple_of((((x + 2) % NX) // 2) * (rows - fk), 128)
    fl = pl.ds(fs, fk)
    over = 2 * fk - rows
    first = lax.broadcasted_iota(jnp.int32, (1, fk), 1) < over
    drop = jnp.logical_and(first, x < 2)

    def scale_f(k):
        half, lo = CUTS[k] // 128, CUTS[k] % 128
        scale_to(ef.at[half, :, fl], 128 + lo, rawf, CUTS[k], CUTS[k + 1] - CUTS[k], mean_l[:, fl],
                 jnp.where(drop, 0.0, inv_l[:, fl]))

    def pass_z(k):
        to_z[k].wait_recv()
        go(to_diag[k])

    def scale_z(k):
        half, lo, n = ZCUTS[k] // 128, ZCUTS[k] % 128, ZCUTS[k + 1] - ZCUTS[k]
        scale(far.at[half, c], lo, raw.at[1], ZCUTS[k], n)
        to_diag[k].wait_recv()
        scale(far.at[half, 1 - c], lo, raw.at[2], ZCUTS[k], n)

    def take_f(*ks):
        for k in ks:
            fwd[k].wait_recv()
            scale_f(k)

    def scale_e(k):
        half, lo, n = CUTS[k] // 128, CUTS[k] % 128, CUTS[k + 1] - CUTS[k]
        to_e[k].wait_recv()
        scale(ef.at[half], lo, rawe, CUTS[k], n)

    def near_own():
        for cc in range(2):
            p = nt(near[cc], near[c])
            for k in range(4):
                ps[0, k, cc] = p[128 * (k // 2):128 * (k // 2) + 128, 128 * (k % 2):128 * (k % 2) + 128]

    def near_ef(g, half):
        for cc in range(2):
            p = nt(near[cc], ef[half])
            for k in range(4):
                ps[g, k, cc] = p[128 * (k // 2):128 * (k // 2) + 128, 128 * (k % 2):128 * (k % 2) + 128]

    def far_with(g, slot, ra, right):
        p = nt(far[ra].reshape(256, rows), right)
        for cc in range(2):
            for k in range(2):
                ps[g, slot + k, cc] = p[128 * cc:128 * cc + 128, 128 * k:128 * k + 128]

    def sum_y_start(g):
        cs[g] = ps[g].astype(BF16)
        go(*sum_y[g])

    sum_y = [[remote(cs.at[g, (y + dy) % NY], rs.at[g, dy - 1], rs_s.at[g], rs_r.at[g],
                     at(l, (y + dy) % NY, h, x, c)) for dy in range(1, NY)] for g in range(EARLY)]
    sum_l = [remote(tmp.at[g, 1 - l], r2.at[g], r2_s.at[g], r2_r.at[g], at(1 - l, y, h, x, c)) for g in range(EARLY)]

    ring3 = [(dl, dy) for dl in range(2) for dy in range(NY) if (dl, dy) != (0, 0)]
    sum_s = {}
    for g in range(EARLY, SETS):
        sum_s[g] = [remote(cs.at[g, (y + dy) % NY, (l + dl) % 2], rd.at[g - EARLY, i], d_s.at[g - EARLY], d_r.at[g - EARLY],
                           at((l + dl) % 2, (y + dy) % NY, h, x, c)) for i, (dl, dy) in enumerate(ring3)]

    def sum_start(g):
        cs[g] = ps[g].astype(BF16)
        go(*sum_s[g])

    def total(g):
        if g < EARLY:
            sum_l[g].wait_recv()
            tot = tmp[g, l] + r2[g]
        else:
            got(rd.at[g - EARLY], d_r.at[g - EARLY])
            tot = ps[g, y, l]
            for i in range(len(ring3)):
                tot = tot + rd[g - EARLY, i].astype(F32)
        return tot * (1.0 / root)

    def sum_l_start(g):
        got(rs.at[g], rs_r.at[g])
        tot = ps[g, y]
        for k in range(NY - 1):
            tot = tot + rs[g, k].astype(F32)
        tmp[g] = tot
        go(sum_l[g])

    def kinds(g):
        if g == 0:
            return [(None, False)]
        if g in MIXED:
            return [(y < 2, False), (y >= 2, True)]
        return [(None, True)]

    def under(cond, fn):
        if cond is None:
            fn()
        else:
            pl.when(cond)(fn)

    def slots(n):
        return cs.at[0] if n == 8 else rd.at[0, pl.ds(0, n)]

    def publish(g):
        zf = g in ZFIRST
        i = (ZFIRST if zf else YFIRST).index(g)
        send, cond_send = (zf_s.at[i, 0], zf_s.at[i, 1]) if zf else (yf_s.at[i, 0], yf_s.at[i, 1])
        recv, recv_t = (zf_r.at[i, 0], zf_r.at[i, 0]) if zf else (yf_r.at[i, 0], yf_r.at[i, 1])
        far_set = role(g, 3)[0]
        spots = [((l + k) % 2, y) for k in range(2)] if zf else [(l, (y + k) % NY) for k in range(NY)]
        tot = total(g)
        pc[g] = tot.astype(BF16)
        if g > 0:
            pt[g] = tot.T.astype(BF16)

        def asis(k, xd):
            return remote(pc.at[g], fin.at[g, y, l], send, recv, at(*spots[k], h, xd, c))

        def turned(k, sem):
            tl, ty = spots[k]
            if far_set and not zf:
                tl = 1 - l
            return remote(pt.at[g], fin.at[g, y, 2 + c], sem, recv_t, at(tl, ty, (h + far_set) % 2, x, l))

        def start(two):
            if not two:
                pltpu.make_async_copy(pc.at[g], fin.at[g, y, l], recv).start()
                for k in range(1, len(spots)):
                    asis(k, x).start()
                return
            for k in range(len(spots)):
                asis(k, (x + 3 - y % 2) % NX).start()
                if k > 0:
                    turned(k, send).start()
            if far_set:
                turned(0, send).start()
            else:
                @pl.when(c == l)
                def _():
                    pltpu.make_async_copy(pt.at[g], fin.at[g, y, 2 + c], recv_t).start()

                @pl.when(c != l)
                def _():
                    turned(0, cond_send).start()

        def sent(two):
            n = 2 * len(spots) if two else len(spots)
            if not two or not far_set:
                n -= 1
            got(slots(n), send)
            if two and not far_set:
                @pl.when(c != l)
                def _():
                    turned(0, cond_send).wait_send()

        for cond, two in kinds(g):
            under(cond, lambda two=two: start(two))
        wait_sent.append(lambda: [under(cond, lambda two=two: sent(two)) for cond, two in kinds(g)])

    wait_sent = []

    def along_y(g, dy):
        i, n = ZFIRST.index(g), 4 if g > 0 else 2
        mine = fin.at[g, y, pl.ds(0, n)]
        return remote(mine, mine, zf_s.at[i, 2], zf_r.at[i, 1], at(l, (y + dy) % NY, h, x, c))

    def spread(g):
        n = 4 if g > 0 else 2
        got(fin.at[g, y, pl.ds(0, n)], zf_r.at[ZFIRST.index(g), 0])
        for dy in range(1, NY):
            along_y(g, dy).start()

    def finish(g):
        i, n = ZFIRST.index(g), 4 if g > 0 else 2
        three = fin.at[g, pl.ds(0, 3), pl.ds(0, n)]
        got(three, zf_r.at[i, 1])
        got(three, zf_s.at[i, 2])

    def across(g, k):
        i = YFIRST.index(g)
        low = 2 if g in MIXED else 0
        view = fin.at[g, pl.ds(0, NY), l] if k == 0 else fin.at[g, pl.ds(low, NY - low), pl.ds(2, 2)]
        return remote(view, view, yf_s.at[i, 2 + k], yf_r.at[i, 2 if k == 0 else 1], at(1 - l, y, h, x, c)), view

    def cross_asis(g):
        cp, view = across(g, 0)
        got(view, yf_r.at[YFIRST.index(g), 0])
        cp.start()

    def first_hand(g):
        return c != l if role(g, 3)[0] else c == l

    def cross_turned(g):
        @pl.when(first_hand(g))
        def _():
            cp, view = across(g, 1)
            got(view, yf_r.at[YFIRST.index(g), 1])
            cp.start()

    def finish_late(g):
        i = YFIRST.index(g)
        got(fin.at[g, pl.ds(0, NY), 1 - l], yf_r.at[i, 2])
        cp, view = across(g, 1)

        @pl.when(jnp.logical_not(first_hand(g)))
        def _():
            got(view, yf_r.at[i, 1])

        @pl.when(first_hand(g))
        def _():
            cp.wait_send()
        across(g, 0)[0].wait_send()

    pass_f(2)
    go(to_e[3], to_e[4], *to_f[3:])
    scale(near.at[c], 0, xt, 0, cols)
    pass_z(0)
    to_core.wait_recv()
    scale(near.at[1 - c], 0, raw.at[0], 0, cols)
    near_own()
    sum_y_start(0)
    redp[...] = nt(kept[...], near[c])
    dsend = []
    for i, (dl, dy) in enumerate(ring3):
        tl, ty = (l + dl) % 2, (y + dy) % NY
        dsend.append(remote(redp.at[pl.ds(pl.multiple_of((tl * NY + ty) * 8, 8), 8)], redr.at[i], d_s.at[3], d_r.at[3],
                            at(tl, ty, h, x, c)))
    scale_e(0)
    scale_e(1)
    scale_z(0)
    pass_z(1)
    sum_l_start(0)
    go(to_z[3], to_e[5], to_e[6])
    scale_e(2)
    take_f(0, 1, 2)
    near_ef(1, 0)
    sum_y_start(1)
    scale_z(1)
    far_with(2, 0, 0, near[c])
    far_with(2, 2, 0, ef[0])
    sum_y_start(2)
    publish(0)
    go(to_z[4])
    pass_f(3)
    pass_z(2)
    scale_e(3)
    scale_z(2)
    pass_f(4)
    sum_l_start(1)
    pass_z(3)
    pass_f(5)
    scale_z(3)
    sum_l_start(2)
    go(to_z[5])
    pass_f(6)
    scale_e(4)
    spread(0)
    take_f(3, 4)
    publish(1)
    publish(2)
    scale_e(5)
    scale_e(6)
    pass_z(4)
    take_f(5, 6)
    near_ef(3, 1)
    sum_start(3)
    scale_z(4)
    far_with(4, 0, 0, ef[1])
    pass_z(5)
    go(*dsend)
    scale_z(5)
    far_with(4, 2, 1, ef[0])
    sum_start(4)
    far_with(5, 0, 1, near[c])
    far_with(5, 2, 1, ef[1])
    publish(3)
    sum_start(5)
    cross_asis(1)
    spread(3)
    publish(4)
    cross_turned(1)
    cross_asis(2)
    publish(5)
    cross_turned(2)
    spread(4)
    cross_asis(5)
    cross_turned(5)
    got(redr, d_r.at[3])
    tot = redp[pl.ds(pl.multiple_of(s * 8, 8), 8), :]
    for i in range(len(ring3)):
        tot = tot + redr[i]
    red_ref[...] = tot
    for g in range(SETS):
        (finish_late if g in YFIRST else finish)(g)

    for fn in wait_sent:
        fn()
    own_f = remote(xt.at[:, pl.ds(fs_mine, fk)], relay, bulk_s.at[0], bulk_r.at[0], left)
    own_f.wait_send()
    for ref, k in ((xt, 1), (xt, 2), (xt, 3), (xt, 4), (relay, 5)):
        got(ref, bulk_s.at[k])
    got(got1, st_s.at[0])
    got(got2, st_s.at[1])
    for g in range(EARLY):
        got(rs.at[g], rs_s.at[g])
        sum_l[g].wait_send()
    for g in range(SETS - EARLY):
        got(rd.at[g], d_s.at[g])
    got(redr, d_s.at[3])


def assemble(fin, red_in, gram, red_ref, block, out_sem):
    _, _, h, x, _ = place()
    red_ref[...] = red_in[...]

    def tile(step, nf, half, row, col):
        return step, (h + nf) % 2, pl.ds(half * 256 + row * 128, 128), pl.ds(col * 128, 128)

    def store(step, half):
        return pltpu.make_async_copy(block.at[step, half], gram.at[half, (x + step) % NX], out_sem.at[2 * step + half])

    for step in (0, 1, 3, 2):
        for g in range(SETS):
            for y in range(NY):
                nf, kind, ra, cb = role(g, y)
                for j in range(2):
                    if kind == step:
                        block[tile(step, nf, j, ra, cb)] = fin[g, y, j].astype(F32)
                    if kind == 1 and step == 3:
                        block[tile(step, nf, j, cb, ra)] = fin[g, y, 2 + j].astype(F32)
        if step == 2:
            for g in range(SETS):
                for y in range(NY):
                    nf, kind, ra, cb = role(g, y)
                    if kind == 2:
                        for j in range(2):
                            block[tile(step, nf, j, cb, ra)] += fin[g, y, 2 + j].astype(F32)
        for half in range(2):
            store(step, half).start()
    for step in range(NX):
        for half in range(2):
            store(step, half).wait()


def local(snapshots, var_index, modes, retained):
    rows, cols = snapshots.shape
    n_space, n_time = lax.axis_size("space"), lax.axis_size("tm")
    total_rows = rows * n_space
    count = float(total_rows // VARS * (cols * n_time))
    root = float(total_rows) ** 0.5
    r = modes.shape[1]
    fk = (rows // 128 + 1) // 2 * 128
    dma = pltpu.SemaphoreType.DMA

    def body(*refs):
        kernel(count, root, fk, *refs)

    vmem = pl.BlockSpec(memory_space=pltpu.VMEM)
    fin, red = pl.pallas_call(
        body,
        name="gram",
        out_shape=(pltpu.VMEM((SETS, NY, 4, 128, 128), BF16), pltpu.VMEM((r // n_space, cols), F32)),
        in_specs=[pl.BlockSpec(memory_space=pltpu.HBM)] * 3 + [pl.BlockSpec(memory_space=pltpu.SMEM)],
        out_specs=(vmem, vmem),
        scratch_shapes=[
            pltpu.VMEM((rows, cols), BF16),
            pltpu.VMEM((rows,), jnp.int32),
            pltpu.VMEM((r, rows), BF16),
            dma((4,)),
            pltpu.VMEM((cols, rows), BF16),
            pltpu.VMEM((3, cols, rows), BF16),
            pltpu.VMEM((cols, rows), BF16),
            pltpu.VMEM((cols, fk), BF16),
            pltpu.VMEM((cols, fk), BF16),
            pltpu.VMEM((2, cols, rows), BF16),
            pltpu.VMEM((2, 2, 128, rows), BF16),
            pltpu.VMEM((2, 256, rows), BF16),
            pltpu.VMEM((VARS, rows), F32),
            pltpu.VMEM((1, rows), F32),
            pltpu.VMEM((1, rows), F32),
            pltpu.VMEM((r, rows), BF16),
            pltpu.VMEM((VARS, 128), F32),
            pltpu.VMEM((VARS, 128), F32),
            pltpu.VMEM((7, VARS, 128), F32),
            pltpu.VMEM((15, VARS, 128), F32),
            pltpu.VMEM((SETS, NY, 2, 128, 128), F32),
            pltpu.VMEM((SETS, NY, 2, 128, 128), BF16),
            pltpu.VMEM((EARLY, NY - 1, 2, 128, 128), BF16),
            pltpu.VMEM((EARLY, 2, 128, 128), F32),
            pltpu.VMEM((EARLY, 128, 128), F32),
            pltpu.VMEM((r, cols), F32),
            pltpu.VMEM((7, 8, cols), F32),
            pltpu.VMEM((SETS, 128, 128), BF16),
            pltpu.VMEM((SETS, 128, 128), BF16),
            pltpu.VMEM((SETS - EARLY, 7, 128, 128), BF16),
            dma((6,)), dma((3 * (len(CUTS) - 1) + 2 * (len(ZCUTS) - 1) + 1,)), dma((2,)), dma((2,)),
            dma((EARLY,)), dma((EARLY,)), dma((EARLY,)), dma((EARLY,)), dma((4,)), dma((4,)),
            dma((3, 3)), dma((3, 2)), dma((3, 4)), dma((3, 3)),
        ],
        compiler_params=pltpu.CompilerParams(
            collective_id=0, has_side_effects=True, vmem_limit_bytes=59 * 2 ** 20),
    )(snapshots, var_index, modes.T, retained)
    gram, red = pl.pallas_call(
        assemble,
        name="columns",
        in_specs=[vmem, vmem],
        out_specs=(pl.BlockSpec(memory_space=pl.ANY), vmem),
        out_shape=(jax.ShapeDtypeStruct((2, NX, 2 * cols, cols), F32), jax.ShapeDtypeStruct(red.shape, F32)),
        scratch_shapes=[pltpu.VMEM((NX, 2, 2 * cols, cols), F32), dma((2 * NX,))],
        compiler_params=pltpu.CompilerParams(vmem_limit_bytes=40 * 2 ** 20),
    )(fin, red)
    return gram.reshape(cols * n_time, cols), red


def solution(mesh):
    return jax.shard_map(
        local,
        mesh=mesh,
        in_specs=(P("space", "tm"), P("space"), P("space", None), P()),
        out_specs=(P(None, "tm"), P("space", "tm")),
        check_vma=False,
    )
```

```python
import jax
import jax.numpy as jnp
from jax import lax
from jax.experimental import pallas as pl
from jax.experimental.pallas import tpu as pltpu
from jax.sharding import PartitionSpec as P

MESH = pl.DeviceIdType.MESH
VARS = 8
NY, NX = 4, 4
F32, BF16 = jnp.float32, jnp.bfloat16


def place():
    s, t = lax.axis_index("space"), lax.axis_index("tm")
    return s // NY, s % NY, t // 8, (t // 2) % NX, t % 2


def at(l, y, h, x, c):
    return (l * NY + y, h * 8 + x * 2 + c)


def nt(a, b):
    return lax.dot_general(a, b, (((1,), (1,)), ((), ())), preferred_element_type=F32)


def pack(n, total, squares):
    lane = lax.broadcasted_iota(jnp.int32, (VARS, 128), 1)
    return jnp.where(lane == 0, n, jnp.where(lane == 1, total, squares))


def merge(tiles):
    n = sum(t[:, 0:1] for t in tiles)
    total = sum(t[:, 1:2] for t in tiles)
    mean = total / jnp.maximum(n, 1.0)
    squares = jnp.zeros_like(n)
    for t in tiles:
        off = t[:, 1:2] / jnp.maximum(t[:, 0:1], 1.0) - mean
        squares = squares + t[:, 2:3] + t[:, 0:1] * off * off
    return n, total, squares


def role(g, y):
    two, odd = y // 2, y % 2
    if g == 0:
        return 0, 0, two, odd
    if g in (1, 3):
        return 0, 1 + odd, two, g // 2
    if g == 4:
        return 1, 1 + odd, two, 1 - two
    last = g // 3
    return (1, 0, last, odd) if two == 0 else (1, 1 + odd, last, last)


SETS = 6
MIXED = (2, 5)
EARLY = 3
YFIRST = (1, 2, 5)
ZFIRST = (0, 3, 4)
CUTS = (0, 16, 64, 128, 160, 192, 224, 256)
ZCUTS = (0, 64, 128, 160, 192, 224, 256)


def kernel(count, root, fk, x_hbm, vi_hbm, modes_hbm, ret_ref, fin, red_ref,
           x_ref, vi_ref, modes_ref, load, xt, raw, rawe, relay, rawf, near, far, ef, hot, mean_l, inv_l, kept,
           tile1, tile2, got1, got2, ps, cs, rs, tmp, r2, redp, redr, pc, pt,
           rd, bulk_s, bulk_r, st_s, st_r, rs_s, rs_r, r2_s, r2_r, d_s, d_r, zf_s, zf_r, yf_s, yf_r):
    l, y, h, x, c = place()
    s = l * NY + y
    rows = xt.shape[1]
    cols = xt.shape[0]
    ntile = rows // 128

    ring1 = [(dx, dc) for dx in range(NX) for dc in range(2) if (dx, dc) != (0, 0)]
    ring2 = [(dy, dl, dh) for dy in range(NY) for dl in range(2) for dh in range(2) if (dy, dl, dh) != (0, 0, 0)]

    def dev1(dx, dc):
        return at(l, y, h, (x + dx) % NX, (c + dc) % 2)

    def dev2(dy, dl, dh):
        return at((l + dl) % 2, (y + dy) % NY, (h + dh) % 2, x, c)

    lanes = [pl.ds(128 * half, 128) for half in range(2)]
    x_loads = [pltpu.make_async_copy(x_hbm.at[:, r], x_ref.at[:, r], load.at[half]) for half, r in enumerate(lanes)]
    vi_load = pltpu.make_async_copy(vi_hbm, vi_ref, load.at[2])
    modes_load = pltpu.make_async_copy(modes_hbm, modes_ref, load.at[3])
    for cp in x_loads + [vi_load, modes_load]:
        cp.start()
    barrier = pltpu.get_barrier_semaphore()
    for d in ring1:
        pl.semaphore_signal(barrier, inc=1, device_id=dev1(*d), device_id_type=MESH)
    for d in ring2:
        pl.semaphore_signal(barrier, inc=1, device_id=dev2(*d), device_id_type=MESH)

    def turn(half):
        x_loads[half].wait()
        for k in range(ntile):
            xt[128 * half:128 * half + 128, 128 * k:128 * k + 128] = x_ref[128 * k:128 * k + 128, 128 * half:128 * half + 128].T

    turn(0)
    pl.semaphore_wait(barrier, len(ring1) + len(ring2))

    def remote(src, dst, ss, rsem, dev):
        return pltpu.make_async_remote_copy(src, dst, ss, rsem, device_id=dev, device_id_type=MESH)

    def go(*copies):
        for cp in copies:
            cp.start()

    def got(ref, sem):
        pltpu.make_async_copy(ref, ref, sem).wait()

    fs_mine = pl.multiple_of((x // 2) * (rows - fk), 128)
    parts = [pl.ds(lo, hi - lo) for lo, hi in zip(CUTS, CUTS[1:])]
    to_f, to_e, to_z, to_core, to_diag, fwd = [], [], [], [], [], []
    left, core = at(l, y, h, (x + NX - 1) % NX, c), at(l, y, h, x, 1 - c)
    nf, nz = len(CUTS) - 1, len(ZCUTS) - 1
    for k, r in enumerate(parts):
        to_f.append(remote(xt.at[r, pl.ds(fs_mine, fk)], relay.at[r], bulk_s.at[0], bulk_r.at[k], left))
        to_e.append(remote(xt.at[r], rawe.at[r], bulk_s.at[1], bulk_r.at[nf + k], at(l, y, h, (x + 1) % NX, c)))
        fwd.append(remote(relay.at[r], rawf.at[r], bulk_s.at[5], bulk_r.at[2 * nf + k], left))
    for k, r in enumerate([pl.ds(lo, hi - lo) for lo, hi in zip(ZCUTS, ZCUTS[1:])]):
        to_z.append(remote(xt.at[r], raw.at[1, r], bulk_s.at[2], bulk_r.at[3 * nf + k], at(l, y, 1 - h, x, c)))
        to_diag.append(remote(raw.at[1, r], raw.at[2, r], bulk_s.at[4], bulk_r.at[3 * nf + nz + k], core))
    to_core = remote(xt, raw.at[0], bulk_s.at[3], bulk_r.at[3 * nf + 2 * nz], core)

    def pass_f(*ks):
        for k in ks:
            to_f[k].wait_recv()
            go(fwd[k])

    go(to_f[0], to_e[0], to_z[0])
    turn(1)
    go(to_core)

    vi_load.wait()
    hot[...] = (vi_ref[...][None, :] == lax.broadcasted_iota(jnp.int32, (VARS, rows), 0)).astype(F32)

    def colsum(fn):
        def body(k, acc):
            blk = xt[pl.ds(pl.multiple_of(k * 16, 16), 16), :].astype(F32)
            return acc + fn(blk)
        acc = lax.fori_loop(0, cols // 16, body, jnp.zeros((16, rows), F32))
        return jnp.sum(acc, axis=0, keepdims=True)

    n1 = jnp.sum(hot[...], axis=1, keepdims=True) * cols
    sum1 = jnp.sum(hot[...] * colsum(lambda b: b), axis=1, keepdims=True)
    m1 = sum1 / jnp.maximum(n1, 1.0)
    mean_l[...] = jnp.sum(hot[...] * m1, axis=0, keepdims=True)

    def sq(b):
        d = b - mean_l[...]
        return d * d
    sq1 = jnp.sum(hot[...] * colsum(sq), axis=1, keepdims=True)
    tile1[...] = pack(n1, sum1, sq1)
    sends1 = [remote(tile1, got1.at[i], st_s.at[0], st_r.at[0], dev1(*d)) for i, d in enumerate(ring1)]
    go(*sends1)
    go(to_f[1], to_e[1], to_f[2], to_e[2])
    modes_load.wait()
    keep = lax.broadcasted_iota(jnp.int32, kept.shape, 0) < ret_ref[0]
    kept[...] = jnp.where(keep, modes_ref[...].astype(F32), 0.0).astype(BF16)
    for half in range(2):
        ef[half, 128:256, :] = jnp.zeros((128, rows), BF16)
    got(got1, st_r.at[0])
    pass_f(0)
    n2, sum2, sq2 = merge([tile1[...]] + [got1[i] for i in range(len(ring1))])
    tile2[...] = pack(n2, sum2, sq2)
    sends2 = [remote(tile2, got2.at[i], st_s.at[1], st_r.at[1], dev2(*d)) for i, d in enumerate(ring2)]
    go(*sends2)
    go(to_z[1])
    pass_f(1)
    got(got2, st_r.at[1])
    _, sum3, sq3 = merge([tile2[...]] + [got2[i] for i in range(len(ring2))])
    mean = sum3 / count
    inv = 1.0 / jnp.sqrt(sq3 / count + 1e-06)
    mean_l[...] = jnp.sum(hot[...] * mean, axis=0, keepdims=True)
    inv_l[...] = jnp.sum(hot[...] * inv, axis=0, keepdims=True)
    go(to_z[2])

    def scale_to(dst, dlo, src, lo, n, m, v):
        def body(k, _):
            a = pl.multiple_of(k * 16, 16)
            dst[pl.ds(dlo + a, 16), :] = ((src[pl.ds(lo + a, 16), :].astype(F32) - m) * v).astype(BF16)
            return 0
        lax.fori_loop(0, n // 16, body, 0)

    def scale(dst, dlo, src, lo, n):
        scale_to(dst, dlo, src, lo, n, mean_l[...], inv_l[...])

    fs = pl.multiple_of((((x + 2) % NX) // 2) * (rows - fk), 128)
    fl = pl.ds(fs, fk)
    over = 2 * fk - rows
    first = lax.broadcasted_iota(jnp.int32, (1, fk), 1) < over
    drop = jnp.logical_and(first, x < 2)

    def scale_f(k):
        half, lo = CUTS[k] // 128, CUTS[k] % 128
        scale_to(ef.at[half, :, fl], 128 + lo, rawf, CUTS[k], CUTS[k + 1] - CUTS[k], mean_l[:, fl],
                 jnp.where(drop, 0.0, inv_l[:, fl]))

    def pass_z(k):
        to_z[k].wait_recv()
        go(to_diag[k])

    def scale_z(k):
        half, lo, n = ZCUTS[k] // 128, ZCUTS[k] % 128, ZCUTS[k + 1] - ZCUTS[k]
        scale(far.at[half, c], lo, raw.at[1], ZCUTS[k], n)
        to_diag[k].wait_recv()
        scale(far.at[half, 1 - c], lo, raw.at[2], ZCUTS[k], n)

    def take_f(*ks):
        for k in ks:
            fwd[k].wait_recv()
            scale_f(k)

    def scale_e(k):
        half, lo, n = CUTS[k] // 128, CUTS[k] % 128, CUTS[k + 1] - CUTS[k]
        to_e[k].wait_recv()
        scale(ef.at[half], lo, rawe, CUTS[k], n)

    def near_own():
        for cc in range(2):
            p = nt(near[cc], near[c])
            for k in range(4):
                ps[0, k, cc] = p[128 * (k // 2):128 * (k // 2) + 128, 128 * (k % 2):128 * (k % 2) + 128]

    def near_ef(g, half):
        for cc in range(2):
            p = nt(near[cc], ef[half])
            for k in range(4):
                ps[g, k, cc] = p[128 * (k // 2):128 * (k // 2) + 128, 128 * (k % 2):128 * (k % 2) + 128]

    def far_with(g, slot, ra, right):
        p = nt(far[ra].reshape(256, rows), right)
        for cc in range(2):
            for k in range(2):
                ps[g, slot + k, cc] = p[128 * cc:128 * cc + 128, 128 * k:128 * k + 128]

    def sum_y_start(g):
        cs[g] = ps[g].astype(BF16)
        go(*sum_y[g])

    sum_y = [[remote(cs.at[g, (y + dy) % NY], rs.at[g, dy - 1], rs_s.at[g], rs_r.at[g],
                     at(l, (y + dy) % NY, h, x, c)) for dy in (2, 1, 3)] for g in range(EARLY)]
    sum_l = [remote(tmp.at[g, 1 - l], r2.at[g], r2_s.at[g], r2_r.at[g], at(1 - l, y, h, x, c)) for g in range(EARLY)]

    ring3 = [(1, 2), (1, 1), (1, 3), (1, 0), (0, 2), (0, 1), (0, 3)]
    sum_s = {}
    for g in range(EARLY, SETS):
        sum_s[g] = [remote(cs.at[g, (y + dy) % NY, (l + dl) % 2], rd.at[g - EARLY, i], d_s.at[g - EARLY], d_r.at[g - EARLY],
                           at((l + dl) % 2, (y + dy) % NY, h, x, c)) for i, (dl, dy) in enumerate(ring3)]

    def sum_start(g):
        cs[g] = ps[g].astype(BF16)
        go(*sum_s[g])

    def total(g):
        if g < EARLY:
            sum_l[g].wait_recv()
            tot = tmp[g, l] + r2[g]
        else:
            got(rd.at[g - EARLY], d_r.at[g - EARLY])
            tot = ps[g, y, l]
            for i in range(len(ring3)):
                tot = tot + rd[g - EARLY, i].astype(F32)
        return tot * (1.0 / root)

    def sum_l_start(g):
        got(rs.at[g], rs_r.at[g])
        tot = ps[g, y]
        for k in range(NY - 1):
            tot = tot + rs[g, k].astype(F32)
        tmp[g] = tot
        go(sum_l[g])

    def kinds(g):
        if g == 0:
            return [(None, False)]
        if g in MIXED:
            return [(y < 2, False), (y >= 2, True)]
        return [(None, True)]

    def under(cond, fn):
        if cond is None:
            fn()
        else:
            pl.when(cond)(fn)

    def slots(n):
        return cs.at[0] if n == 8 else rd.at[0, pl.ds(0, n)]

    def publish(g):
        zf = g in ZFIRST
        i = (ZFIRST if zf else YFIRST).index(g)
        send, cond_send = (zf_s.at[i, 0], zf_s.at[i, 1]) if zf else (yf_s.at[i, 0], yf_s.at[i, 1])
        recv, recv_t = (zf_r.at[i, 0], zf_r.at[i, 0]) if zf else (yf_r.at[i, 0], yf_r.at[i, 1])
        far_set = role(g, 3)[0]
        spots = [((l + k) % 2, y) for k in range(2)] if zf else [(l, (y + k) % NY) for k in range(NY)]
        tot = total(g)
        pc[g] = tot.astype(BF16)
        if g > 0:
            pt[g] = tot.T.astype(BF16)

        def asis(k, xd):
            return remote(pc.at[g], fin.at[g, y, l], send, recv, at(*spots[k], h, xd, c))

        def turned(k, sem):
            tl, ty = spots[k]
            if far_set and not zf:
                tl = 1 - l
            return remote(pt.at[g], fin.at[g, y, 2 + c], sem, recv_t, at(tl, ty, (h + far_set) % 2, x, l))

        def start(two):
            if not two:
                pltpu.make_async_copy(pc.at[g], fin.at[g, y, l], recv).start()
                for k in range(1, len(spots)):
                    asis(k, x).start()
                return
            for k in range(len(spots)):
                asis(k, (x + 3 - y % 2) % NX).start()
                if k > 0:
                    turned(k, send).start()
            if far_set:
                turned(0, send).start()
            else:
                @pl.when(c == l)
                def _():
                    pltpu.make_async_copy(pt.at[g], fin.at[g, y, 2 + c], recv_t).start()

                @pl.when(c != l)
                def _():
                    turned(0, cond_send).start()

        def sent(two):
            n = 2 * len(spots) if two else len(spots)
            if not two or not far_set:
                n -= 1
            got(slots(n), send)
            if two and not far_set:
                @pl.when(c != l)
                def _():
                    turned(0, cond_send).wait_send()

        for cond, two in kinds(g):
            under(cond, lambda two=two: start(two))
        wait_sent.append(lambda: [under(cond, lambda two=two: sent(two)) for cond, two in kinds(g)])

    wait_sent = []

    def along_y(g, dy):
        i, n = ZFIRST.index(g), 4 if g > 0 else 2
        mine = fin.at[g, y, pl.ds(0, n)]
        return remote(mine, mine, zf_s.at[i, 2], zf_r.at[i, 1], at(l, (y + dy) % NY, h, x, c))

    def spread(g):
        n = 4 if g > 0 else 2
        got(fin.at[g, y, pl.ds(0, n)], zf_r.at[ZFIRST.index(g), 0])
        for dy in (2, 1, 3):
            along_y(g, dy).start()

    def finish(g):
        i, n = ZFIRST.index(g), 4 if g > 0 else 2
        three = fin.at[g, pl.ds(0, 3), pl.ds(0, n)]
        got(three, zf_r.at[i, 1])
        got(three, zf_s.at[i, 2])

    def across(g, k):
        i = YFIRST.index(g)
        low = 2 if g in MIXED else 0
        view = fin.at[g, pl.ds(0, NY), l] if k == 0 else fin.at[g, pl.ds(low, NY - low), pl.ds(2, 2)]
        return remote(view, view, yf_s.at[i, 2 + k], yf_r.at[i, 2 if k == 0 else 1], at(1 - l, y, h, x, c)), view

    def cross_asis(g):
        cp, view = across(g, 0)
        got(view, yf_r.at[YFIRST.index(g), 0])
        cp.start()

    def first_hand(g):
        return c != l if role(g, 3)[0] else c == l

    def cross_turned(g):
        @pl.when(first_hand(g))
        def _():
            cp, view = across(g, 1)
            got(view, yf_r.at[YFIRST.index(g), 1])
            cp.start()

    def finish_late(g):
        i = YFIRST.index(g)
        got(fin.at[g, pl.ds(0, NY), 1 - l], yf_r.at[i, 2])
        cp, view = across(g, 1)

        @pl.when(jnp.logical_not(first_hand(g)))
        def _():
            got(view, yf_r.at[i, 1])

        @pl.when(first_hand(g))
        def _():
            cp.wait_send()
        across(g, 0)[0].wait_send()

    pass_f(2)
    go(to_e[3], to_e[4], *to_f[3:])
    scale(near.at[c], 0, xt, 0, cols)
    pass_z(0)
    to_core.wait_recv()
    scale(near.at[1 - c], 0, raw.at[0], 0, cols)
    near_own()
    sum_y_start(0)
    redp[...] = nt(kept[...], near[c])
    dsend = []
    for i, (dl, dy) in enumerate(ring3):
        tl, ty = (l + dl) % 2, (y + dy) % NY
        dsend.append(remote(redp.at[pl.ds(pl.multiple_of((tl * NY + ty) * 8, 8), 8)], redr.at[i], d_s.at[3], d_r.at[3],
                            at(tl, ty, h, x, c)))
    scale_e(0)
    scale_e(1)
    scale_z(0)
    pass_z(1)
    sum_l_start(0)
    go(to_z[3], to_e[5], to_e[6])
    scale_e(2)
    take_f(0, 1, 2)
    near_ef(1, 0)
    sum_y_start(1)
    scale_z(1)
    far_with(2, 0, 0, near[c])
    far_with(2, 2, 0, ef[0])
    sum_y_start(2)
    publish(0)
    go(to_z[4])
    pass_f(3)
    pass_z(2)
    scale_e(3)
    scale_z(2)
    pass_f(4)
    sum_l_start(1)
    pass_z(3)
    pass_f(5)
    scale_z(3)
    sum_l_start(2)
    go(to_z[5])
    pass_f(6)
    scale_e(4)
    spread(0)
    take_f(3, 4)
    publish(1)
    publish(2)
    scale_e(5)
    scale_e(6)
    pass_z(4)
    take_f(5, 6)
    near_ef(3, 1)
    sum_start(3)
    scale_z(4)
    far_with(4, 0, 0, ef[1])
    pass_z(5)
    go(*dsend)
    scale_z(5)
    far_with(4, 2, 1, ef[0])
    sum_start(4)
    far_with(5, 0, 1, near[c])
    far_with(5, 2, 1, ef[1])
    publish(3)
    sum_start(5)
    cross_asis(1)
    spread(3)
    publish(4)
    cross_turned(1)
    cross_asis(2)
    publish(5)
    cross_turned(2)
    spread(4)
    cross_asis(5)
    cross_turned(5)
    got(redr, d_r.at[3])
    tot = redp[pl.ds(pl.multiple_of(s * 8, 8), 8), :]
    for i in range(len(ring3)):
        tot = tot + redr[i]
    red_ref[...] = tot
    for g in range(SETS):
        (finish_late if g in YFIRST else finish)(g)

    for fn in wait_sent:
        fn()
    own_f = remote(xt.at[:, pl.ds(fs_mine, fk)], relay, bulk_s.at[0], bulk_r.at[0], left)
    own_f.wait_send()
    for ref, k in ((xt, 1), (xt, 2), (xt, 3), (xt, 4), (relay, 5)):
        got(ref, bulk_s.at[k])
    got(got1, st_s.at[0])
    got(got2, st_s.at[1])
    for g in range(EARLY):
        got(rs.at[g], rs_s.at[g])
        sum_l[g].wait_send()
    for g in range(SETS - EARLY):
        got(rd.at[g], d_s.at[g])
    got(redr, d_s.at[3])


def assemble(fin, red_in, gram, red_ref, block, out_sem):
    _, _, h, x, _ = place()
    red_ref[...] = red_in[...]

    def tile(step, nf, half, row, col):
        return step, (h + nf) % 2, pl.ds(half * 256 + row * 128, 128), pl.ds(col * 128, 128)

    def store(step, half):
        return pltpu.make_async_copy(block.at[step, half], gram.at[half, (x + step) % NX], out_sem.at[2 * step + half])

    for step in (0, 1, 3, 2):
        for g in range(SETS):
            for y in range(NY):
                nf, kind, ra, cb = role(g, y)
                for j in range(2):
                    if kind == step:
                        block[tile(step, nf, j, ra, cb)] = fin[g, y, j].astype(F32)
                    if kind == 1 and step == 3:
                        block[tile(step, nf, j, cb, ra)] = fin[g, y, 2 + j].astype(F32)
        if step == 2:
            for g in range(SETS):
                for y in range(NY):
                    nf, kind, ra, cb = role(g, y)
                    if kind == 2:
                        for j in range(2):
                            block[tile(step, nf, j, cb, ra)] += fin[g, y, 2 + j].astype(F32)
        for half in range(2):
            store(step, half).start()
    for step in range(NX):
        for half in range(2):
            store(step, half).wait()


def local(snapshots, var_index, modes, retained):
    rows, cols = snapshots.shape
    n_space, n_time = lax.axis_size("space"), lax.axis_size("tm")
    total_rows = rows * n_space
    count = float(total_rows // VARS * (cols * n_time))
    root = float(total_rows) ** 0.5
    r = modes.shape[1]
    fk = (rows // 128 + 1) // 2 * 128
    dma = pltpu.SemaphoreType.DMA

    def body(*refs):
        kernel(count, root, fk, *refs)

    vmem = pl.BlockSpec(memory_space=pltpu.VMEM)
    fin, red = pl.pallas_call(
        body,
        name="gram",
        out_shape=(pltpu.VMEM((SETS, NY, 4, 128, 128), BF16), pltpu.VMEM((r // n_space, cols), F32)),
        in_specs=[pl.BlockSpec(memory_space=pltpu.HBM)] * 3 + [pl.BlockSpec(memory_space=pltpu.SMEM)],
        out_specs=(vmem, vmem),
        scratch_shapes=[
            pltpu.VMEM((rows, cols), BF16),
            pltpu.VMEM((rows,), jnp.int32),
            pltpu.VMEM((r, rows), BF16),
            dma((4,)),
            pltpu.VMEM((cols, rows), BF16),
            pltpu.VMEM((3, cols, rows), BF16),
            pltpu.VMEM((cols, rows), BF16),
            pltpu.VMEM((cols, fk), BF16),
            pltpu.VMEM((cols, fk), BF16),
            pltpu.VMEM((2, cols, rows), BF16),
            pltpu.VMEM((2, 2, 128, rows), BF16),
            pltpu.VMEM((2, 256, rows), BF16),
            pltpu.VMEM((VARS, rows), F32),
            pltpu.VMEM((1, rows), F32),
            pltpu.VMEM((1, rows), F32),
            pltpu.VMEM((r, rows), BF16),
            pltpu.VMEM((VARS, 128), F32),
            pltpu.VMEM((VARS, 128), F32),
            pltpu.VMEM((7, VARS, 128), F32),
            pltpu.VMEM((15, VARS, 128), F32),
            pltpu.VMEM((SETS, NY, 2, 128, 128), F32),
            pltpu.VMEM((SETS, NY, 2, 128, 128), BF16),
            pltpu.VMEM((EARLY, NY - 1, 2, 128, 128), BF16),
            pltpu.VMEM((EARLY, 2, 128, 128), F32),
            pltpu.VMEM((EARLY, 128, 128), F32),
            pltpu.VMEM((r, cols), F32),
            pltpu.VMEM((7, 8, cols), F32),
            pltpu.VMEM((SETS, 128, 128), BF16),
            pltpu.VMEM((SETS, 128, 128), BF16),
            pltpu.VMEM((SETS - EARLY, 7, 128, 128), BF16),
            dma((6,)), dma((3 * (len(CUTS) - 1) + 2 * (len(ZCUTS) - 1) + 1,)), dma((2,)), dma((2,)),
            dma((EARLY,)), dma((EARLY,)), dma((EARLY,)), dma((EARLY,)), dma((4,)), dma((4,)),
            dma((3, 3)), dma((3, 2)), dma((3, 4)), dma((3, 3)),
        ],
        compiler_params=pltpu.CompilerParams(
            collective_id=0, has_side_effects=True, vmem_limit_bytes=59 * 2 ** 20),
    )(snapshots, var_index, modes.T, retained)
    gram, red = pl.pallas_call(
        assemble,
        name="columns",
        in_specs=[vmem, vmem],
        out_specs=(pl.BlockSpec(memory_space=pl.ANY), vmem),
        out_shape=(jax.ShapeDtypeStruct((2, NX, 2 * cols, cols), F32), jax.ShapeDtypeStruct(red.shape, F32)),
        scratch_shapes=[pltpu.VMEM((NX, 2, 2 * cols, cols), F32), dma((2 * NX,))],
        compiler_params=pltpu.CompilerParams(vmem_limit_bytes=40 * 2 ** 20),
    )(fin, red)
    return gram.reshape(cols * n_time, cols), red


def solution(mesh):
    return jax.shard_map(
        local,
        mesh=mesh,
        in_specs=(P("space", "tm"), P("space"), P("space", None), P()),
        out_specs=(P(None, "tm"), P("space", "tm")),
        check_vma=False,
    )
```
